256 devices in a mesh: box: 16 (over x, y), row: 16 (over z, core).
Axes of the slice: x: 4, y: 4, z: 8, core: 2. Of those that a mesh axis runs over, the one named last changes fastest.
Arguments:
- child_maps: float32 [2, 32, 1024, 1024], P(None, 'box', 'row'), may hold values from -1 to 1
- child_faces: int32 [32, 1024], replicated, may hold values from -1 to 511, as said below
- parent_faces: int32 [16, 1024], replicated, may hold values from -1 to 511, as said below
Outputs:
- parent_maps: float32 [2, 16, 1024, 1024], P(None, 'box', 'row')
- grand_maps: float32 [2, 1024, 8192], P(None, 'row', 'box')
The draws below stay inside these ranges and needn't reach their ends.
Inputs may be any that keep to these rules, and one draw needn't show every extreme that they name: `child_faces`: in each row, every face position 0 to 511 occurs exactly once, and each aligned block of 32 nodes holds exactly 16 shared nodes. `parent_faces`: in each row, every face position 0 to 511 occurs exactly once, and each aligned block of 32 nodes holds exactly 16 shared nodes.
All inputs are finite; a program needn't handle non-finite values.
Results may differ from the reference program's by a relative error of at most 0.00012.
Values sent between devices are 32-bit elements; how exact they have to be, the bound alone decides.
A program may use at most 128 MiB of HBM per device.

```python
import math
import jax
import jax.numpy as jnp
from jax import lax

ORDER = 1024
NODE_BLOCK = 32
TERMS = 4
BOXES = 32
SHARED = 512
EXTERIOR = 512


def face_table(key, amount):
    blocks = ORDER // NODE_BLOCK
    score_key, shuffle_key = jax.random.split(key)
    scores = jax.random.randint(score_key, (amount, blocks, NODE_BLOCK), 0, 1 << 20) * NODE_BLOCK
    scores = scores + jnp.arange(NODE_BLOCK, dtype=jnp.int32)
    ranking = jnp.sum((scores[..., None, :] < scores[..., :, None]).astype(jnp.int32), axis=-1)
    shared = (ranking < NODE_BLOCK // 2).reshape(amount, ORDER)
    positions = jnp.cumsum(shared.astype(jnp.int32), axis=1) - 1
    shuffles = jax.vmap(lambda single: jax.random.permutation(single, ORDER // 2))(jax.random.split(shuffle_key, amount))
    faces = jnp.take_along_axis(shuffles.astype(jnp.int32), jnp.clip(positions, 0, ORDER // 2 - 1), axis=1)
    return jnp.where(shared, faces, -1).astype(jnp.int32)


def draw_child_faces(key, part):
    key = jax.random.fold_in(key, 11)
    return face_table(key, BOXES)


def draw_parent_faces(key, part):
    key = jax.random.fold_in(key, 12)
    return face_table(key, BOXES // 2)


def draw_child_maps(key, part):
    key = jax.random.fold_in(key, 13)
    noise_key, size_key, angle_key, row_key, column_key, phase_key = jax.random.split(key, 6)
    shape = (2, BOXES, ORDER, ORDER)
    noise = jax.random.normal(noise_key, shape, jnp.float32)
    dense_weight = 0.93
    lowest = 0.01
    highest_size = 0.03
    noise_norm = 0.03
    noise = noise * (noise_norm / (2.0 * math.sqrt(2.0 * ORDER)))
    row_order = jax.vmap(lambda single: jax.random.permutation(single, ORDER))(jax.random.split(row_key, BOXES)).astype(jnp.int32)
    column_order = jax.vmap(lambda single: jax.random.permutation(single, ORDER))(jax.random.split(column_key, BOXES)).astype(jnp.int32)
    turns = row_order[:, :, None] * column_order[:, None, :] % ORDER
    phases = jax.random.uniform(phase_key, (2, BOXES, ORDER), jnp.float32, -math.pi, math.pi)
    dense_angle = turns.astype(jnp.float32) * (2.0 * math.pi / ORDER) + phases[0][:, :, None] + phases[1][:, None, :]
    dense = dense_weight / math.sqrt(ORDER) * jnp.stack([jnp.cos(dense_angle), jnp.sin(dense_angle)])
    magnitude = jnp.exp(jax.random.uniform(size_key, (BOXES, ORDER), jnp.float32, math.log(lowest), math.log(highest_size)))
    angle = jax.random.uniform(angle_key, (BOXES, ORDER), jnp.float32, -math.pi, math.pi)
    diagonal = jnp.stack([magnitude * jnp.cos(angle), magnitude * jnp.sin(angle)])
    identity = jnp.eye(ORDER, dtype=jnp.float32)
    return dense + noise * (1.0 - identity) + diagonal[..., None] * identity


def setup_inputs(seed: int = 0) -> dict:
    key_list = jax.random.split(jax.random.key(seed), 4)
    return {
        "child_maps": draw_child_maps(jax.random.fold_in(key_list[3], 71), 0),
        "child_faces": draw_child_faces(jax.random.fold_in(key_list[3], 71), 0),
        "parent_faces": draw_parent_faces(jax.random.fold_in(key_list[3], 71), 0),
    }


highest = lax.Precision.HIGHEST


def real_dot(factor, operand):
    return jnp.dot(factor, operand, precision=highest, preferred_element_type=jnp.float32)


def complex_product(factor, operand):
    real_part = real_dot(factor[0], operand[0]) - real_dot(factor[1], operand[1])
    imag_part = real_dot(factor[0], operand[1]) + real_dot(factor[1], operand[0])
    return jnp.stack([real_part, imag_part])


def node_list(marked, amount):
    ranking = jnp.cumsum(marked.astype(jnp.int32)) - 1
    target = jnp.where(marked, ranking, amount).astype(jnp.int32)
    node_ids = jnp.arange(marked.shape[0], dtype=jnp.int32)
    return jnp.zeros((amount,), jnp.int32).at[target].set(node_ids, mode="drop")


def alternate(former, latter, dimension):
    block_width = NODE_BLOCK // 2
    first_moved = jnp.moveaxis(former, dimension, -1)
    second_moved = jnp.moveaxis(latter, dimension, -1)
    leading = first_moved.shape[:-1]
    blocks = first_moved.shape[-1] // block_width
    joined = jnp.stack([first_moved.reshape(leading + (blocks, block_width)),
                        second_moved.reshape(leading + (blocks, block_width))], axis=-2)
    return jnp.moveaxis(joined.reshape(leading + (2 * first_moved.shape[-1],)), -1, dimension)


def face_lists(alpha_faces, beta_faces):
    alpha_shared = node_list(alpha_faces >= 0, SHARED)
    alpha_outer = node_list(alpha_faces < 0, EXTERIOR)
    beta_outer = node_list(beta_faces < 0, EXTERIOR)
    wanted_faces = jnp.take(alpha_faces, alpha_shared)
    node_ids = jnp.arange(beta_faces.shape[0], dtype=jnp.int32)
    face_target = jnp.where(beta_faces >= 0, beta_faces, SHARED).astype(jnp.int32)
    face_owner = jnp.zeros((SHARED,), jnp.int32).at[face_target].set(node_ids, mode="drop")
    beta_slots = jnp.take(face_owner, wanted_faces).astype(jnp.int32)
    return alpha_shared, alpha_outer, beta_outer, beta_slots


def merge_maps(alpha_map, beta_map, alpha_faces, beta_faces):
    alpha_shared, alpha_outer, beta_outer, beta_slots = face_lists(alpha_faces, beta_faces)
    alpha_face_rows = jnp.take(alpha_map, alpha_shared, axis=1)
    alpha_outer_rows = jnp.take(alpha_map, alpha_outer, axis=1)
    beta_face_rows = jnp.take(beta_map, beta_slots, axis=1)
    beta_outer_rows = jnp.take(beta_map, beta_outer, axis=1)
    alpha_inner = jnp.take(alpha_face_rows, alpha_shared, axis=2)
    alpha_part = jnp.take(alpha_face_rows, alpha_outer, axis=2)
    alpha_cross = alternate(alpha_part, jnp.zeros_like(alpha_part), 2)
    beta_inner = jnp.take(beta_face_rows, beta_slots, axis=2)
    beta_part = jnp.take(beta_face_rows, beta_outer, axis=2)
    beta_cross = alternate(jnp.zeros_like(beta_part), beta_part, 2)
    alpha_couple = jnp.take(alpha_outer_rows, alpha_shared, axis=2)
    beta_couple = jnp.take(beta_outer_rows, beta_slots, axis=2)
    alpha_block = jnp.take(alpha_outer_rows, alpha_outer, axis=2)
    beta_block = jnp.take(beta_outer_rows, beta_outer, axis=2)
    outer_alpha = alternate(alpha_block, jnp.zeros_like(alpha_block), 2)
    outer_beta = alternate(jnp.zeros_like(beta_block), beta_block, 2)
    interface = complex_product(alpha_inner, beta_inner)
    loading = alpha_cross - complex_product(alpha_inner, beta_cross)
    solution = loading
    for counter in range(TERMS - 1):
        solution = loading + complex_product(interface, solution)
    through = beta_cross - complex_product(beta_inner, solution)
    upper = outer_alpha - complex_product(alpha_couple, through)
    lower = outer_beta - complex_product(beta_couple, solution)
    return alternate(upper, lower, 1)


def reference(child_maps, child_faces, parent_faces):
    parents = []
    for parent in range(BOXES // 2):
        group_index = parent // 2
        parity = parent % 2
        alpha_box = 4 * group_index + parity
        beta_box = alpha_box + 2
        parents.append(merge_maps(child_maps[:, alpha_box], child_maps[:, beta_box],
                                  child_faces[alpha_box], child_faces[beta_box]))
    parent_maps = jnp.stack(parents, axis=1)
    grands = []
    for group_index in range(BOXES // 4):
        grands.append(merge_maps(parent_maps[:, 2 * group_index], parent_maps[:, 2 * group_index + 1],
                                 parent_faces[2 * group_index], parent_faces[2 * group_index + 1]))
    return parent_maps, jnp.concatenate(grands, axis=2)
```

```python
import functools

import jax
import jax.numpy as jnp
from jax import lax
from jax.experimental import pallas as pl
from jax.experimental.pallas import tpu as pltpu
from jax.sharding import PartitionSpec as P

MESH = pl.DeviceIdType.MESH
F32 = jnp.float32
BF16 = jnp.bfloat16
ORDER = 1024
SHARED = 512
RING = 16
PER_SECTION = 17
PER_LEVEL = 4 * PER_SECTION + 4
TOTAL = 2 * PER_LEVEL


def dot(a, b):
    return jnp.dot(a, b, preferred_element_type=F32)


def dot_nt(a, b):
    return lax.dot_general(a, b, (((1,), (1,)), ((), ())), preferred_element_type=F32)


def split(x):
    hi = x.astype(BF16)
    return hi, (x - hi.astype(F32)).astype(BF16)


def iota(shape, dim):
    return lax.broadcasted_iota(jnp.int32, shape, dim)


def one_hot(mask):
    return jnp.where(mask, 1.0, 0.0).astype(BF16)


def prefix_counts(rows):
    width = rows.shape[1]
    lower = one_hot(iota((width, width), 0) < iota((width, width), 1))
    return dot(jnp.where(rows < 0, 1.0, 0.0).astype(BF16), lower).astype(jnp.int32)


def chunked(faces):
    return jnp.concatenate([faces[:, 256 * t : 256 * t + 256] for t in range(4)], axis=0)


def build_selectors(own, other, local, face_ref, outer_ref):
    rows = jnp.concatenate([chunked(own), chunked(other)], axis=0)
    counts = prefix_counts(rows)
    lane = iota((1, 256), 1)
    slot = iota((128, 256), 0)
    own_value = own.astype(F32)
    for t in range(4):
        outer_rank = jnp.where(rows[t : t + 1] < 0, counts[t : t + 1], -1)
        outer_ref[t] = one_hot(outer_rank == slot)
        face_row = rows[4 + t : 5 + t]
        shared_rank = jnp.where(face_row < 0, -1, lane - counts[4 + t : 5 + t])
        wanted = jnp.sum(
            jnp.where(shared_rank == slot, face_row.astype(F32), 0.0), axis=1, keepdims=True
        )
        face_ref[128 * t : 128 * t + 128, :] = one_hot(own_value == wanted)
    count = prefix_counts(jnp.broadcast_to(local, (8, 64)))[0:1]
    target = jnp.where(local < 0, 32 + count, iota((1, 64), 1) - count)
    return one_hot(target == iota((64, 64), 0))


def select(parts, row_hot, face_ref, outer_ref):
    stack = []
    for value in parts:
        for piece in split(value):
            stack.append(dot(row_hot, piece).astype(BF16))
    stack = jnp.concatenate(stack, axis=0)
    face = dot_nt(stack, face_ref[...])
    outer = jnp.concatenate(
        [dot_nt(stack[:, 256 * t : 256 * t + 256], outer_ref[t]) for t in range(4)], axis=1
    )
    face = [face[0:64] + face[64:128], face[128:192] + face[192:256]]
    outer = [outer[0:64] + outer[64:128], outer[128:192] + outer[192:256]]
    return face, outer


def complex_product(x, w):
    m = x[0].shape[0]
    hi, lo = split(jnp.concatenate(x, axis=0))
    both = jnp.concatenate([hi, lo], axis=0)
    sums = []
    for part in range(2):
        main = dot(both, w[0, part])
        sums.append(main[: 2 * m] + main[2 * m :] + dot(hi, w[1, part]))
    by_real, by_imag = sums
    return [by_real[:m] - by_imag[m:], by_imag[:m] + by_real[m:]]


def convert(gathered, pieces, role):
    @pl.loop(0, RING)
    def _(k):
        rows = pl.ds(pl.multiple_of(k * 32, 32), 32)
        for part in range(2):
            hi, lo = split(gathered[role, k, part])
            pieces[role, 0, part, rows, :] = hi
            pieces[role, 1, part, rows, :] = lo


def weave(alpha, beta):
    return jnp.concatenate([alpha[0:16], beta[0:16], alpha[16:32], beta[16:32]], axis=0)


def kernel(
    maps_ref, child_faces_ref, parent_faces_ref, parent_ref, grand_ref,
    ss1, sx1, xs1, xx1, ss2, sx2, xs2, xx2, out_ss, out_sx, out_xs, out_xx, out_sx2, out_xx2,
    face_hot, outer_hot, face_hot2, outer_hot2, wss, wsx, wsx2, send, recv,
):
    box, row = lax.axis_index("box"), lax.axis_index("row")
    par = lax.rem(box, 2)
    mate = box + 1 - 2 * par
    core = lax.rem(row, 2)
    z = lax.div(row, 2)
    sib = row + 1 - 2 * core
    up, down = lax.rem(row + 2, RING), lax.rem(row + RING - 2, RING)
    to_up, to_down, to_sib, to_mate = (box, up), (box, down), (box, sib), (mate, row)

    barrier = pltpu.get_barrier_semaphore()
    for target in (to_up, to_down, to_sib, to_mate):
        pl.semaphore_signal(barrier, inc=1, device_id=target, device_id_type=MESH)

    pending = []

    def copy(src, dst, target, k):
        return pltpu.make_async_remote_copy(
            src_ref=src, dst_ref=dst, send_sem=send.at[k], recv_sem=recv.at[k],
            device_id=target, device_id_type=MESH,
        )

    def push(src, dst, target, k):
        c = copy(src, dst, target, k)
        c.start()
        pending.append(c)

    def arrived(dst, k):
        copy(dst, dst, to_mate, k).wait_recv()

    def section_id(level, kind, q):
        return level * PER_LEVEL + (2 * kind + q) * PER_SECTION

    def mate_id(level, i):
        return level * PER_LEVEL + 4 * PER_SECTION + i

    def back(base, hops):
        return lax.rem(base + 2 * RING - 2 * hops, RING)

    def start(buf, role, sid):
        own = buf.at[role, row]
        push(own, own, to_up, sid)
        push(own, own, to_down, sid + 4)
        push(own, own, to_sib, sid + 8)

    def step(buf, role, sid, j):
        for way, target, half in ((0, to_up, 0), (1, to_down, 1)):
            block = buf.at[role, back(row, (j + 1) if way == 0 else -(j + 1))]
            arrived(block, sid + 4 * way + j)
            onward = block if j < 2 else block.at[half]
            push(onward, onward, target, sid + 4 * way + j + 1)
            push(block, block, to_sib, sid + 9 + 3 * way + j)

    def last(buf, role, sid):
        for way in range(2):
            half = buf.at[role, back(row, 4), way]
            arrived(half, sid + 4 * way + 3)
            push(half, half, to_sib, sid + 15 + way)

    def sibling_done(buf, role, sid):
        arrived(buf.at[role, sib], sid + 8)
        for way in range(2):
            for j in range(3):
                block = buf.at[role, back(sib, (j + 1) if way == 0 else -(j + 1))]
                arrived(block, sid + 9 + 3 * way + j)
            arrived(buf.at[role, back(sib, 4), way], sid + 15 + way)

    def faces_of(ref, i):
        group = pl.ds(pl.multiple_of(8 * lax.div(i, 8), 8), 8)
        lanes = pl.ds(pl.multiple_of(z * 128, 128), 128)
        inside = lax.rem(i, 8)
        whole = jnp.sum(
            jnp.where(iota((8, ORDER), 0) == inside, ref[group, :], 0), axis=0, keepdims=True
        )
        chunk = jnp.sum(
            jnp.where(iota((8, 128), 0) == inside, ref[group, lanes], 0), axis=0, keepdims=True
        )
        local = jnp.where(core == 0, chunk[:, :64], chunk[:, 64:])
        return whole, local

    first = 2 * (box - par)

    other_role = 1 - par
    own_faces, local = faces_of(child_faces_ref, first + 1 + par)
    paired, _ = faces_of(child_faces_ref, first + 3 - 3 * par)
    hot = build_selectors(own_faces, paired, local, face_hot, outer_hot)
    face, outer = select(
        [maps_ref[part, other_role] for part in range(2)], hot, face_hot, outer_hot
    )
    for part in range(2):
        out_ss[part] = face[part][:32]
        out_xs[part] = face[part][32:]
        out_sx[part] = outer[part][:32]
        out_xx[part] = outer[part][32:]
    pl.semaphore_wait(barrier, 4)
    push(out_ss, ss1.at[par, row], to_mate, mate_id(0, 0))
    push(out_sx, sx1.at[par, row], to_mate, mate_id(0, 1))
    push(out_xs, xs1.at[par], to_mate, mate_id(0, 2))
    push(out_xx, xx1.at[par], to_mate, mate_id(0, 3))

    own_faces, local = faces_of(child_faces_ref, first + 3 * par)
    paired, _ = faces_of(child_faces_ref, first + 2 - par)
    hot = build_selectors(own_faces, paired, local, face_hot, outer_hot)
    face, outer = select([maps_ref[part, par] for part in range(2)], hot, face_hot, outer_hot)
    for part in range(2):
        ss1[par, row, part] = face[part][:32]
        xs1[par, part] = face[part][32:]
        sx1[par, row, part] = outer[part][:32]
        xx1[par, part] = outer[part][32:]

    def merge(level, ss, sx, xs, xx, wx, emit, between):
        roles = (par, 1 - par)
        s_ids = [section_id(level, 0, q) for q in range(2)]
        x_ids = [section_id(level, 1, q) for q in range(2)]
        start(ss, roles[0], s_ids[0])
        arrived(ss.at[1 - par, row], mate_id(level, 0))
        start(ss, roles[1], s_ids[1])
        between()
        for j in range(3):
            for q in range(2):
                step(ss, roles[q], s_ids[q], j)
            if j == 1:
                start(sx, roles[0], x_ids[0])
                arrived(sx.at[1 - par, row], mate_id(level, 1))
                start(sx, roles[1], x_ids[1])
        for q in range(2):
            last(ss, roles[q], s_ids[q])
        arrived(xs.at[1 - par], mate_id(level, 2))
        arrived(xx.at[1 - par], mate_id(level, 3))
        for q in range(2):
            step(sx, roles[q], x_ids[q], 0)
        for q in range(2):
            sibling_done(ss, roles[q], s_ids[q])
        convert(ss, wss, 1)
        u = [xs[0, part] for part in range(2)]
        lead = complex_product(u, wss.at[1])
        base = [jnp.concatenate([lead[part], -xs[1, part]], axis=0) for part in range(2)]
        convert(ss, wss, 0)
        w = base
        for term in range(3):
            t = complex_product(w, wss.at[0])
            if term < 2:
                step(sx, roles[0], x_ids[0], 1 + term)
            else:
                last(sx, roles[0], x_ids[0])
            t = complex_product(t, wss.at[1])
            w = [base[part] + t[part] for part in range(2)]
            if term < 2:
                step(sx, roles[1], x_ids[1], 1 + term)
            else:
                last(sx, roles[1], x_ids[1])
        t = complex_product(w, wss.at[0])
        t = [jnp.concatenate([t[part][:32] + u[part], t[part][32:]], axis=0) for part in range(2)]
        for q in range(2):
            sibling_done(sx, roles[q], x_ids[q])
        convert(sx, wx, 0)
        alpha = complex_product(w, wx.at[0])
        convert(sx, wx, 1)
        beta = complex_product(t, wx.at[1])
        width = alpha[0].shape[1]
        stack = []
        for part in range(2):
            left = weave(xx[0, part] + alpha[part][:32], alpha[part][32:])
            right = weave(-beta[part][:32], xx[1, part] - beta[part][32:])
            stack.append((left, right))
        rank, place = iota((256, 256), 0), iota((256, 256), 1)
        inside = jnp.where(rank < 128, rank, rank - 128)
        spot = 32 * lax.div(inside, 16) + lax.rem(inside, 16) + jnp.where(rank < 128, 0, 16)
        place_hot = one_hot(spot == place)
        for tile in range(width // 128):
            cols = slice(128 * tile, 128 * tile + 128)
            packed = jnp.concatenate(
                [
                    jnp.concatenate([stack[part][0][:, cols], stack[part][1][:, cols]], axis=1)
                    for part in range(2)
                ],
                axis=0,
            )
            hi, lo = split(packed)
            spread = dot(jnp.concatenate([hi, lo], axis=0), place_hot)
            spread = spread[:128] + spread[128:]
            for part in range(2):
                emit(part, tile, spread[64 * part : 64 * part + 64])

    def emit_parent(part, tile, value):
        parent_ref[part, 0, :, 256 * tile : 256 * tile + 256] = value

    def emit_grand(part, tile, value):
        grand_ref[part, :, 256 * tile : 256 * tile + 256] = value

    hots = []

    def prepare():
        own, loc = faces_of(parent_faces_ref, box)
        pair, _ = faces_of(parent_faces_ref, mate)
        hots.append(build_selectors(own, pair, loc, face_hot2, outer_hot2))

    merge(0, ss1, sx1, xs1, xx1, wsx, emit_parent, prepare)

    face, outer = select([parent_ref[part, 0] for part in range(2)], hots[0], face_hot2, outer_hot2)
    for part in range(2):
        ss2[par, row, part] = face[part][:32]
        xs2[par, part] = face[part][32:]
        halves = [outer[part][:, :256], outer[part][:, 256:]]
        mine = jnp.where(par == 0, halves[0], halves[1])
        theirs = jnp.where(par == 0, halves[1], halves[0])
        sx2[par, row, part] = mine[:32]
        xx2[par, part] = mine[32:]
        out_sx2[part] = theirs[:32]
        out_xx2[part] = theirs[32:]
    push(ss2.at[par, row], ss2.at[par, row], to_mate, mate_id(1, 0))
    push(out_sx2, sx2.at[par, row], to_mate, mate_id(1, 1))
    push(xs2.at[par], xs2.at[par], to_mate, mate_id(1, 2))
    push(out_xx2, xx2.at[par], to_mate, mate_id(1, 3))
    merge(1, ss2, sx2, xs2, xx2, wsx2, emit_grand, lambda: None)

    for c in pending:
        c.wait_send()


def per_device(child_maps, child_faces, parent_faces):
    def vmem(*shape, dtype=F32):
        return pltpu.VMEM(shape, dtype)

    whole = pl.BlockSpec(memory_space=pltpu.VMEM)
    return pl.pallas_call(
        kernel,
        out_shape=(
            jax.ShapeDtypeStruct((2, 1, 64, ORDER), F32),
            jax.ShapeDtypeStruct((2, 64, SHARED), F32),
        ),
        in_specs=[whole] * 3,
        out_specs=(whole, whole),
        scratch_shapes=[
            vmem(2, RING, 2, 32, 512), vmem(2, RING, 2, 32, 512), vmem(2, 2, 32, 512), vmem(2, 2, 32, 512),
            vmem(2, RING, 2, 32, 512), vmem(2, RING, 2, 32, 256), vmem(2, 2, 32, 512), vmem(2, 2, 32, 256),
            vmem(2, 32, 512), vmem(2, 32, 512), vmem(2, 32, 512), vmem(2, 32, 512),
            vmem(2, 32, 256), vmem(2, 32, 256),
            vmem(512, 1024, dtype=BF16), vmem(4, 128, 256, dtype=BF16),
            vmem(512, 1024, dtype=BF16), vmem(4, 128, 256, dtype=BF16),
            vmem(2, 2, 2, 512, 512, dtype=BF16),
            vmem(2, 2, 2, 512, 512, dtype=BF16),
            vmem(2, 2, 2, 512, 256, dtype=BF16),
            pltpu.SemaphoreType.DMA((TOTAL,)),
            pltpu.SemaphoreType.DMA((TOTAL,)),
        ],
        compiler_params=pltpu.CompilerParams(
            collective_id=0, has_side_effects=True, vmem_limit_bytes=50 * 1024 * 1024
        ),
    )(child_maps, child_faces, parent_faces)


def solution(mesh):
    placed = (P(None, "box", "row", None), P(), P())
    return jax.shard_map(
        per_device,
        mesh=mesh,
        in_specs=placed,
        out_specs=(P(None, "box", "row", None), P(None, "row", "box")),
        check_vma=False,
    )
```

```python
import functools

import jax
import jax.numpy as jnp
from jax import lax
from jax.experimental import pallas as pl
from jax.experimental.pallas import tpu as pltpu
from jax.sharding import PartitionSpec as P

MESH = pl.DeviceIdType.MESH
F32 = jnp.float32
BF16 = jnp.bfloat16
ORDER = 1024
SHARED = 512
RING = 16
TOTAL = 192
DEPTHS = (4, 4)


def order_parent(ssm, sso, sxm, sxo):
    return [
        (ssm, 0), (sxm, 0), (sso, 0), (ssm, 1), (sso, 1), (sxo, 0), (ssm, 2), (sso, 2),
        (sxm, 1), (ssm, 3), (sso, 3), (sxo, 1), (sxm, 2), (sxo, 2), (sxm, 3), (sxo, 3),
    ]


def order_grand(ssi, ssr, sso, sxm, sxo):
    return [
        (ssi, 0), (ssr, 0), (sxm, 0), (sso, 0), (ssi, 1), (ssr, 1), (sso, 1), (ssi, 2), (ssr, 2),
        (sxm, 1), (sso, 2), (ssi, 3), (ssr, 3), (sxo, 0), (sso, 3), (sxm, 2), (sxo, 1), (sxm, 3),
        (sxo, 2), (sxo, 3),
    ]


def dot(a, b):
    return jnp.dot(a, b, preferred_element_type=F32)


def dot_nt(a, b):
    return lax.dot_general(a, b, (((1,), (1,)), ((), ())), preferred_element_type=F32)


def split(x):
    hi = x.astype(BF16)
    return hi, (x - hi.astype(F32)).astype(BF16)


def iota(shape, dim):
    return lax.broadcasted_iota(jnp.int32, shape, dim)


def one_hot(mask):
    return jnp.where(mask, 1.0, 0.0).astype(BF16)


def prefix_counts(rows):
    width = rows.shape[1]
    lower = one_hot(iota((width, width), 0) < iota((width, width), 1))
    return dot(jnp.where(rows < 0, 1.0, 0.0).astype(BF16), lower).astype(jnp.int32)


def chunked(faces):
    return jnp.concatenate([faces[:, 256 * t : 256 * t + 256] for t in range(4)], axis=0)


def build_selectors(own, other, local, face_ref, outer_ref):
    rows = jnp.concatenate([chunked(own), chunked(other)], axis=0)
    counts = prefix_counts(rows)
    lane = iota((1, 256), 1)
    slot = iota((128, 256), 0)
    own_value = own.astype(F32)
    for t in range(4):
        outer_rank = jnp.where(rows[t : t + 1] < 0, counts[t : t + 1], -1)
        outer_ref[t] = one_hot(outer_rank == slot)
        face_row = rows[4 + t : 5 + t]
        shared_rank = jnp.where(face_row < 0, -1, lane - counts[4 + t : 5 + t])
        wanted = jnp.sum(
            jnp.where(shared_rank == slot, face_row.astype(F32), 0.0), axis=1, keepdims=True
        )
        face_ref[128 * t : 128 * t + 128, :] = one_hot(own_value == wanted)
    count = prefix_counts(jnp.broadcast_to(local, (8, 64)))[0:1]
    target = jnp.where(local < 0, 32 + count, iota((1, 64), 1) - count)
    return one_hot(target == iota((64, 64), 0))


def select(parts, row_hot, face_ref, outer_ref):
    stack = []
    for value in parts:
        for piece in split(value):
            stack.append(dot(row_hot, piece).astype(BF16))
    stack = jnp.concatenate(stack, axis=0)
    face = dot_nt(stack, face_ref[...])
    outer = jnp.concatenate(
        [dot_nt(stack[:, 256 * t : 256 * t + 256], outer_ref[t]) for t in range(4)], axis=1
    )
    face = [face[0:64] + face[64:128], face[128:192] + face[192:256]]
    outer = [outer[0:64] + outer[64:128], outer[128:192] + outer[192:256]]
    return face, outer


def complex_product(x, w):
    m = x[0].shape[0]
    hi, lo = split(jnp.concatenate(x, axis=0))
    both = jnp.concatenate([hi, lo], axis=0)
    sums = []
    for part in range(2):
        main = dot(both, w[0, part])
        sums.append(main[: 2 * m] + main[2 * m :] + dot(hi, w[1, part]))
    by_real, by_imag = sums
    return [by_real[:m] - by_imag[m:], by_imag[:m] + by_real[m:]]


def convert(gathered, pieces, role):
    @pl.loop(0, RING)
    def _(k):
        rows = pl.ds(pl.multiple_of(k * 32, 32), 32)
        for part in range(2):
            hi, lo = split(gathered[role, k, part])
            pieces[role, 0, part, rows, :] = hi
            pieces[role, 1, part, rows, :] = lo


def weave(alpha, beta):
    return jnp.concatenate([alpha[0:16], beta[0:16], alpha[16:32], beta[16:32]], axis=0)


def kernel(
    maps_ref, child_faces_ref, parent_faces_ref, parent_out, grand_ref,
    maps, child_rows, parent_rows, parent_ref,
    ss1, sx1, xs1, xx1, ss2, sx2, xs2, xx2, out_ss, out_sx, out_xs, out_xx, out_sx2, out_xx2,
    face_hot, outer_hot, face_hot2, outer_hot2, wss, wsx, wsx2, send, recv, local_sem,
):
    box, row = lax.axis_index("box"), lax.axis_index("row")
    par = lax.rem(box, 2)
    mate = box + 1 - 2 * par
    core = lax.rem(row, 2)
    z = lax.div(row, 2)
    sib = row + 1 - 2 * core
    up, down = lax.rem(row + 2, RING), lax.rem(row + RING - 2, RING)
    to_up, to_down, to_sib, to_mate = (box, up), (box, down), (box, sib), (mate, row)

    barrier = pltpu.get_barrier_semaphore()
    for target in (to_up, to_down, to_sib, to_mate):
        pl.semaphore_signal(barrier, inc=1, device_id=target, device_id_type=MESH)

    first = 2 * (box - par)

    def group(i):
        return pl.ds(pl.multiple_of(8 * lax.div(i, 8), 8), 8)

    loads = [
        pltpu.make_async_copy(child_faces_ref.at[group(first)], child_rows, local_sem.at[0]),
        pltpu.make_async_copy(maps_ref.at[:, 1 - par], maps.at[1], local_sem.at[1]),
        pltpu.make_async_copy(maps_ref.at[:, par], maps.at[0], local_sem.at[2]),
        pltpu.make_async_copy(parent_faces_ref.at[group(box)], parent_rows, local_sem.at[3]),
    ]
    for c in loads:
        c.start()

    ids = {}
    pending = []

    def copy(src, dst, target, key):
        k = ids.setdefault(key, len(ids))
        return pltpu.make_async_remote_copy(
            src_ref=src, dst_ref=dst, send_sem=send.at[k], recv_sem=recv.at[k],
            device_id=target, device_id_type=MESH,
        )

    def push(src, dst, target, key):
        c = copy(src, dst, target, key)
        c.start()
        pending.append(c)

    def arrived(dst, key):
        copy(dst, dst, to_mate, key).wait_recv()

    def away(base, way, hops):
        return lax.rem(base + 2 * RING + (2 if way else -2) * hops, RING)

    class Section:
        def __init__(self, name, buf, role, part=None, forward=False, source=None):
            self.name, self.buf, self.role = name, buf, role
            self.part, self.forward, self.source = part, forward, source

        def block(self, slot):
            whole = self.buf.at[self.role, slot]
            return whole if self.part is None else whole.at[self.part]

        def piece(self, base, way, hop):
            slot = away(base, way, hop)
            if hop < 3:
                return self.block(slot)
            if self.part is not None:
                return self.buf.at[self.role, slot, self.part, pl.ds(16 * way, 16)]
            return self.buf.at[self.role, slot, way]

        def to_mate(self, slot, what):
            if self.forward:
                block = self.block(slot)
                push(block, block, to_mate, (self.name, "mate", what))

        def send(self, way, hop):
            if hop == 0 and way == 0 and self.source is not None:
                arrived(self.block(row), self.source)
            piece = self.piece(row, way, hop)
            push(piece, piece, to_down if way else to_up, (self.name, way, hop))
            if hop == 0 and way == 1:
                own = self.block(row)
                push(own, own, to_sib, (self.name, "sib", "own"))
                self.to_mate(row, "own")

        def receive(self, way, hop):
            slot = away(row, way, hop + 1)
            if hop < 3:
                piece = self.block(slot)
            else:
                piece = self.piece(away(row, way, 1), way, hop)
            arrived(piece, (self.name, way, hop))
            return slot, piece

        def share(self, way, hop, slot, piece):
            push(piece, piece, to_sib, (self.name, "sib", way, hop))
            if hop < 3:
                self.to_mate(slot, (way, hop))
            elif way == 1:
                self.to_mate(slot, "far")

        def done(self):
            arrived(self.block(sib), (self.name, "sib", "own"))
            for way in range(2):
                for hop in range(3):
                    arrived(self.block(away(sib, way, hop + 1)), (self.name, "sib", way, hop))
                arrived(self.piece(away(sib, way, 1), way, 3), (self.name, "sib", way, 3))

    class Flow:
        def __init__(self, order, depth):
            self.order, self.depth = order, depth
            self.sent = self.got = 0

        def ready(self, got):
            more = []
            while self.sent < len(self.order) and self.sent < got + self.depth:
                section, hop = self.order[self.sent]
                if hop and (section, hop - 1) not in self.order[:got]:
                    break
                more.append((section, hop))
                self.sent += 1
            return more

        def begin(self):
            for section, hop in self.ready(0):
                for way in range(2):
                    section.send(way, hop)

        def advance(self, upto=None):
            upto = self.got + 1 if upto is None else upto
            while self.got < min(upto, len(self.order)):
                section, hop = self.order[self.got]
                following = self.ready(self.got + 1)
                for way in range(2):
                    slot, piece = section.receive(way, hop)
                    for later, later_hop in following:
                        later.send(way, later_hop)
                    section.share(way, hop, slot, piece)
                self.got += 1

        def through(self, section):
            return self.order.index((section, 3)) + 1

    class Mirror:
        def __init__(self, name, mine, buf, role):
            self.name, self.mine, self.buf, self.role = name, mine, buf, role

        def block(self, slot):
            return self.buf.at[self.role, slot, 1]

        def take(self, slot, what):
            block = self.block(slot)
            arrived(block, (self.mine, "mate", what))
            push(block, block, to_sib, (self.name, "sib", what))

        def start(self):
            self.take(row, "own")

        def step(self, j):
            for way in range(2):
                self.take(away(row, way, j + 1), (way, j))

        def last(self):
            self.take(away(row, 0, 4), "far")

        def done(self):
            arrived(self.block(sib), (self.name, "sib", "own"))
            for way in range(2):
                for j in range(3):
                    arrived(self.block(away(sib, way, j + 1)), (self.name, "sib", (way, j)))
            arrived(self.block(away(sib, 0, 4)), (self.name, "sib", "far"))

    def faces_of(rows, i):
        inside = lax.rem(i, 8)
        lanes = pl.ds(pl.multiple_of(z * 128, 128), 128)
        whole = jnp.sum(
            jnp.where(iota((8, ORDER), 0) == inside, rows[...], 0), axis=0, keepdims=True
        )
        chunk = jnp.sum(
            jnp.where(iota((8, 128), 0) == inside, rows[:, lanes], 0), axis=0, keepdims=True
        )
        local = jnp.where(core == 0, chunk[:, :64], chunk[:, 64:])
        return whole, local

    loads[0].wait()
    own_faces, local = faces_of(child_rows, first + 1 + par)
    paired, _ = faces_of(child_rows, first + 3 - 3 * par)
    hot = build_selectors(own_faces, paired, local, face_hot, outer_hot)
    loads[1].wait()
    face, outer = select([maps[1, part] for part in range(2)], hot, face_hot, outer_hot)
    for part in range(2):
        out_ss[part] = face[part][:32]
        out_xs[part] = face[part][32:]
        out_sx[part] = outer[part][:32]
        out_xx[part] = outer[part][32:]
    pl.semaphore_wait(barrier, 4)
    push(out_ss, ss1.at[par, row], to_mate, "ss1")

    own_faces, local = faces_of(child_rows, first + 3 * par)
    paired, _ = faces_of(child_rows, first + 2 - par)
    hot = build_selectors(own_faces, paired, local, face_hot, outer_hot)
    loads[2].wait()
    face, outer = select([maps[0, part] for part in range(2)], hot, face_hot, outer_hot)
    for part in range(2):
        ss1[par, row, part] = face[part][:32]
        xs1[par, part] = face[part][32:]
        sx1[par, row, part] = outer[part][:32]
        xx1[par, part] = outer[part][32:]

    def multiply(ss_mine, ss_other, sx_mine, sx_other, xs, xx, wx, emit, flow):
        more = flow.advance
        convert(ss_mine.buf, wss, 1)
        u = [xs[0, part] for part in range(2)]
        lead = complex_product(u, wss.at[1])
        base = [jnp.concatenate([lead[part], -xs[1, part]], axis=0) for part in range(2)]
        more()
        convert(ss_mine.buf, wss, 0)
        w = base
        for term in range(3):
            t = complex_product(w, wss.at[0])
            more()
            t = complex_product(t, wss.at[1])
            w = [base[part] + t[part] for part in range(2)]
            more()
        t = complex_product(w, wss.at[0])
        t = [jnp.concatenate([t[part][:32] + u[part], t[part][32:]], axis=0) for part in range(2)]
        more(flow.through(sx_mine))
        sx_mine.done()
        convert(sx_mine.buf, wx, par)
        mine = complex_product([jnp.where(par == 0, w[p], t[p]) for p in range(2)], wx.at[par])
        more(flow.through(sx_other))
        sx_other.done()
        convert(sx_mine.buf, wx, 1 - par)
        other = complex_product([jnp.where(par == 0, t[p], w[p]) for p in range(2)], wx.at[1 - par])
        alpha = [jnp.where(par == 0, mine[p], other[p]) for p in range(2)]
        beta = [jnp.where(par == 0, other[p], mine[p]) for p in range(2)]
        width = alpha[0].shape[1]
        stack = []
        for part in range(2):
            left = weave(xx[0, part] + alpha[part][:32], alpha[part][32:])
            right = weave(-beta[part][:32], xx[1, part] - beta[part][32:])
            stack.append((left, right))
        rank, place = iota((256, 256), 0), iota((256, 256), 1)
        inside = jnp.where(rank < 128, rank, rank - 128)
        spot = 32 * lax.div(inside, 16) + lax.rem(inside, 16) + jnp.where(rank < 128, 0, 16)
        place_hot = one_hot(spot == place)
        for tile in range(width // 128):
            cols = slice(128 * tile, 128 * tile + 128)
            packed = jnp.concatenate(
                [
                    jnp.concatenate([stack[part][0][:, cols], stack[part][1][:, cols]], axis=1)
                    for part in range(2)
                ],
                axis=0,
            )
            hi, lo = split(packed)
            spread = dot(jnp.concatenate([hi, lo], axis=0), place_hot)
            spread = spread[:128] + spread[128:]
            for part in range(2):
                emit(part, tile, spread[64 * part : 64 * part + 64])

    def emit_parent(part, tile, value):
        parent_ref[part, :, 256 * tile : 256 * tile + 256] = value

    def emit_grand(part, tile, value):
        grand_ref[part, :, 256 * tile : 256 * tile + 256] = value

    ssm, sso = Section("ssm1", ss1, par), Section("sso1", ss1, 1 - par, source="ss1")
    sxm, sxo = Section("sxm1", sx1, par), Section("sxo1", sx1, 1 - par, source="sx1")
    flow = Flow(order_parent(ssm, sso, sxm, sxo), DEPTHS[0])
    flow.begin()
    loads[3].wait()
    own, loc = faces_of(parent_rows, box)
    pair, _ = faces_of(parent_rows, mate)
    hot2 = build_selectors(own, pair, loc, face_hot2, outer_hot2)
    flow.advance(1)
    push(out_sx, sx1.at[par, row], to_mate, "sx1")
    flow.advance(3)
    push(out_xs, xs1.at[par], to_mate, "xs1")
    push(out_xx, xx1.at[par], to_mate, "xx1")
    flow.advance(max(flow.through(ssm), flow.through(sso)))
    arrived(xs1.at[1 - par], "xs1")
    arrived(xx1.at[1 - par], "xx1")
    ssm.done()
    sso.done()
    multiply(ssm, sso, sxm, sxo, xs1, xx1, wsx, emit_parent, flow)

    face, outer = select([parent_ref[part] for part in range(2)], hot2, face_hot2, outer_hot2)
    for part in range(2):
        ss2[par, row, part] = face[part][:32]
        xs2[par, part] = face[part][32:]
    real = ss2.at[par, row, 0]
    push(real, real, to_mate, "ss2")
    ssi, ssr = Section("ssi2", ss2, par, part=1, forward=True), Section("ssr2", ss2, par, part=0)
    sso = Section("sso2", ss2, 1 - par, part=0, source="ss2")
    mirror = Mirror("mir2", "ssi2", ss2, 1 - par)
    sxm, sxo = Section("sxm2", sx2, par), Section("sxo2", sx2, 1 - par, source="sx2")
    for part in range(2):
        halves = [outer[part][:, :256], outer[part][:, 256:]]
        mine = jnp.where(par == 0, halves[0], halves[1])
        theirs = jnp.where(par == 0, halves[1], halves[0])
        sx2[par, row, part] = mine[:32]
        xx2[par, part] = mine[32:]
        out_sx2[part] = theirs[:32]
        out_xx2[part] = theirs[32:]
    push(out_sx2, sx2.at[par, row], to_mate, "sx2")
    flow = Flow(order_grand(ssi, ssr, sso, sxm, sxo), DEPTHS[1])
    flow.begin()
    store = pltpu.make_async_copy(parent_ref, parent_out.at[:, 0], local_sem.at[4])
    store.start()
    at = [flow.order.index((ssi, hop)) + 1 for hop in range(4)]
    flow.advance(at[0])
    push(xs2.at[par], xs2.at[par], to_mate, "xs2")
    mirror.start()
    flow.advance(at[1])
    mirror.step(0)
    push(out_xx2, xx2.at[par], to_mate, "xx2")
    flow.advance(at[2])
    mirror.step(1)
    flow.advance(max(flow.through(ssi), flow.through(ssr), flow.through(sso)))
    mirror.step(2)
    mirror.last()
    arrived(xs2.at[1 - par], "xs2")
    arrived(xx2.at[1 - par], "xx2")
    ssi.done()
    ssr.done()
    sso.done()
    mirror.done()
    multiply(ssi, sso, sxm, sxo, xs2, xx2, wsx2, emit_grand, flow)

    store.wait()
    for c in pending:
        c.wait_send()


def per_device(child_maps, child_faces, parent_faces):
    def vmem(*shape, dtype=F32):
        return pltpu.VMEM(shape, dtype)

    whole = pl.BlockSpec(memory_space=pltpu.VMEM)
    placed = pl.BlockSpec(memory_space=pltpu.HBM)
    return pl.pallas_call(
        kernel,
        out_shape=(
            jax.ShapeDtypeStruct((2, 1, 64, ORDER), F32),
            jax.ShapeDtypeStruct((2, 64, SHARED), F32),
        ),
        in_specs=[placed] * 3,
        out_specs=(placed, whole),
        scratch_shapes=[
            vmem(2, 2, 64, ORDER), pltpu.VMEM((8, ORDER), jnp.int32), pltpu.VMEM((8, ORDER), jnp.int32),
            vmem(2, 64, ORDER),
            vmem(2, RING, 2, 32, 512), vmem(2, RING, 2, 32, 512), vmem(2, 2, 32, 512), vmem(2, 2, 32, 512),
            vmem(2, RING, 2, 32, 512), vmem(2, RING, 2, 32, 256), vmem(2, 2, 32, 512), vmem(2, 2, 32, 256),
            vmem(2, 32, 512), vmem(2, 32, 512), vmem(2, 32, 512), vmem(2, 32, 512),
            vmem(2, 32, 256), vmem(2, 32, 256),
            vmem(512, 1024, dtype=BF16), vmem(4, 128, 256, dtype=BF16),
            vmem(512, 1024, dtype=BF16), vmem(4, 128, 256, dtype=BF16),
            vmem(2, 2, 2, 512, 512, dtype=BF16),
            vmem(2, 2, 2, 512, 512, dtype=BF16),
            vmem(2, 2, 2, 512, 256, dtype=BF16),
            pltpu.SemaphoreType.DMA((TOTAL,)),
            pltpu.SemaphoreType.DMA((TOTAL,)),
            pltpu.SemaphoreType.DMA((5,)),
        ],
        compiler_params=pltpu.CompilerParams(
            collective_id=0, has_side_effects=True, vmem_limit_bytes=58 * 1024 * 1024
        ),
    )(child_maps, child_faces, parent_faces)


def solution(mesh):
    placed = (P(None, "box", "row", None), P(), P())
    return jax.shard_map(
        per_device,
        mesh=mesh,
        in_specs=placed,
        out_specs=(P(None, "box", "row", None), P(None, "row", "box")),
        check_vma=False,
    )
```

```python
import functools

import jax
import jax.numpy as jnp
from jax import lax
from jax.experimental import pallas as pl
from jax.experimental.pallas import tpu as pltpu
from jax.sharding import PartitionSpec as P

MESH = pl.DeviceIdType.MESH
F32 = jnp.float32
BF16 = jnp.bfloat16
ORDER = 1024
SHARED = 512
RING = 16
TOTAL = 208
DEPTHS = (4, 4)


def order_parent(ssm, sso, xa, mb, ob):
    return [
        (ssm, 0), (mb, 0), (sso, 0), (ssm, 1), (xa, 0), (sso, 1), (ssm, 2), (sso, 2), (xa, 1),
        (ssm, 3), (sso, 3), (ob, 0), (mb, 1), (xa, 2), (ob, 1), (mb, 2), (xa, 3), (ob, 2),
        (mb, 3), (ob, 3),
    ]


def order_grand(ssi, ssr, sso, sxm, sxo):
    return [
        (ssi, 0), (ssr, 0), (sso, 0), (ssi, 1), (ssr, 1), (sso, 1), (sxm, 2), (ssi, 2), (ssr, 2),
        (sso, 2), (sxo, 0), (ssi, 3), (ssr, 3), (sso, 3), (sxo, 1), (sxm, 3), (sxo, 2), (sxo, 3),
    ]


def dot(a, b):
    return jnp.dot(a, b, preferred_element_type=F32)


def dot_nt(a, b):
    return lax.dot_general(a, b, (((1,), (1,)), ((), ())), preferred_element_type=F32)


def split(x):
    hi = x.astype(BF16)
    return hi, (x - hi.astype(F32)).astype(BF16)


def iota(shape, dim):
    return lax.broadcasted_iota(jnp.int32, shape, dim)


def one_hot(mask):
    return jnp.where(mask, 1.0, 0.0).astype(BF16)


def prefix_counts(rows):
    width = rows.shape[1]
    lower = one_hot(iota((width, width), 0) < iota((width, width), 1))
    return dot(jnp.where(rows < 0, 1.0, 0.0).astype(BF16), lower).astype(jnp.int32)


def chunked(faces):
    return jnp.concatenate([faces[:, 256 * t : 256 * t + 256] for t in range(4)], axis=0)


def build_selectors(own, other, local, face_ref, outer_ref):
    rows = jnp.concatenate([chunked(own), chunked(other)], axis=0)
    counts = prefix_counts(rows)
    lane = iota((1, 256), 1)
    slot = iota((128, 256), 0)
    own_value = own.astype(F32)
    for t in range(4):
        outer_rank = jnp.where(rows[t : t + 1] < 0, counts[t : t + 1], -1)
        outer_ref[t] = one_hot(outer_rank == slot)
        face_row = rows[4 + t : 5 + t]
        shared_rank = jnp.where(face_row < 0, -1, lane - counts[4 + t : 5 + t])
        wanted = jnp.sum(
            jnp.where(shared_rank == slot, face_row.astype(F32), 0.0), axis=1, keepdims=True
        )
        face_ref[128 * t : 128 * t + 128, :] = one_hot(own_value == wanted)
    count = prefix_counts(jnp.broadcast_to(local, (8, 64)))[0:1]
    target = jnp.where(local < 0, 32 + count, iota((1, 64), 1) - count)
    return one_hot(target == iota((64, 64), 0))


def select_rows(parts, row_hot):
    stack = []
    for value in parts:
        for piece in split(value):
            stack.append(dot(row_hot, piece).astype(BF16))
    return jnp.concatenate(stack, axis=0)


def joined(stack):
    return [stack[0:64] + stack[64:128], stack[128:192] + stack[192:256]]


def pick(par, former, latter):
    return jnp.where(par == 0, former, latter)


def complex_product(x, w):
    m = x[0].shape[0]
    hi, lo = split(jnp.concatenate(x, axis=0))
    both = jnp.concatenate([hi, lo], axis=0)
    sums = []
    for part in range(2):
        main = dot(both, w[0, part])
        sums.append(main[: 2 * m] + main[2 * m :] + dot(hi, w[1, part]))
    by_real, by_imag = sums
    return [by_real[:m] - by_imag[m:], by_imag[:m] + by_real[m:]]


def convert(fetch, pieces):
    @pl.loop(0, RING)
    def _(k):
        rows = pl.ds(pl.multiple_of(k * 32, 32), 32)
        for part in range(2):
            hi, lo = split(fetch(k, part))
            pieces[0, part, rows, :] = hi
            pieces[1, part, rows, :] = lo


def weave(alpha, beta):
    return jnp.concatenate([alpha[0:16], beta[0:16], alpha[16:32], beta[16:32]], axis=0)


def kernel(
    maps_ref, child_faces_ref, parent_faces_ref, parent_out, grand_ref,
    maps, child_rows, parent_rows, parent_ref,
    ss1, sx1a, sx1b, xs1, xx1, ss2, sx2, xs2, xx2, out_ss, out_sx, out_xs, out_xx, out_sx2, out_xx2,
    face_hot, outer_hot, face_hot2, outer_hot2, place_hot, wss, wsx, wsx2, send, recv, local_sem,
):
    box, row = lax.axis_index("box"), lax.axis_index("row")
    par = lax.rem(box, 2)
    mate = box + 1 - 2 * par
    core = lax.rem(row, 2)
    z = lax.div(row, 2)
    sib = row + 1 - 2 * core
    up, down = lax.rem(row + 2, RING), lax.rem(row + RING - 2, RING)
    to_up, to_down, to_sib, to_mate = (box, up), (box, down), (box, sib), (mate, row)

    barrier = pltpu.get_barrier_semaphore()
    for target in (to_up, to_down, to_sib, to_mate):
        pl.semaphore_signal(barrier, inc=1, device_id=target, device_id_type=MESH)

    first = 2 * (box - par)

    def group(i):
        return pl.ds(pl.multiple_of(8 * lax.div(i, 8), 8), 8)

    loads = [
        pltpu.make_async_copy(child_faces_ref.at[group(first)], child_rows, local_sem.at[0]),
        pltpu.make_async_copy(maps_ref.at[:, 1 - par], maps.at[1], local_sem.at[1]),
        pltpu.make_async_copy(maps_ref.at[:, par], maps.at[0], local_sem.at[2]),
        pltpu.make_async_copy(parent_faces_ref.at[group(box)], parent_rows, local_sem.at[3]),
    ]
    for c in loads:
        c.start()

    ids = {}
    pending = []

    def copy(src, dst, target, key):
        k = ids.setdefault(key, len(ids))
        return pltpu.make_async_remote_copy(
            src_ref=src, dst_ref=dst, send_sem=send.at[k], recv_sem=recv.at[k],
            device_id=target, device_id_type=MESH,
        )

    def push(src, dst, target, key):
        c = copy(src, dst, target, key)
        c.start()
        pending.append(c)

    def drain(spare):
        while len(pending) > spare:
            pending.pop(0).wait_send()

    def arrived(dst, key):
        copy(dst, dst, to_mate, key).wait_recv()

    def away(base, way, hops):
        return lax.rem(base + 2 * RING + (2 if way else -2) * hops, RING)

    class Section:
        settled = -1

        def __init__(self, name, buf, part=None, forward=False, source=None):
            self.name, self.buf, self.part, self.forward, self.source = name, buf, part, forward, source

        def block(self, slot):
            return self.buf.at[slot] if self.part is None else self.buf.at[slot, self.part]

        def piece(self, base, way, hop):
            slot = away(base, way, hop)
            if hop < 3:
                return self.block(slot)
            if self.part is not None:
                return self.buf.at[slot, self.part, pl.ds(16 * way, 16)]
            return self.buf.at[slot, way]

        def to_mate(self, slot, what):
            if self.forward:
                block = self.block(slot)
                push(block, block, to_mate, (self.name, "mate", what))

        def send(self, way, hop):
            if hop == 0 and way == 0 and self.source is not None:
                arrived(*self.source)
            piece = self.piece(row, way, hop)
            push(piece, piece, to_down if way else to_up, (self.name, way, hop))
            if hop == 0 and way == 1:
                own = self.block(row)
                push(own, own, to_sib, (self.name, "sib", "own"))
                self.to_mate(row, "own")

        def receive(self, way, hop):
            slot = away(row, way, hop + 1)
            if hop < 3:
                piece = self.block(slot)
            else:
                piece = self.piece(away(row, way, 1), way, hop)
            arrived(piece, (self.name, way, hop))
            return slot, piece

        def share(self, way, hop, slot, piece):
            push(piece, piece, to_sib, (self.name, "sib", way, hop))
            if hop < 3:
                self.to_mate(slot, (way, hop))
            elif way == 1:
                self.to_mate(slot, "far")

        def settle(self, hop):
            while self.settled <= hop:
                if self.settled < 0:
                    arrived(self.block(sib), (self.name, "sib", "own"))
                else:
                    for way in range(2):
                        if self.settled < 3:
                            piece = self.block(away(sib, way, self.settled + 1))
                        else:
                            piece = self.piece(away(sib, way, 1), way, 3)
                        arrived(piece, (self.name, "sib", way, self.settled))
                self.settled += 1

        def done(self):
            self.settle(3)

    class Flow:
        def __init__(self, order, depth):
            self.order, self.depth = order, depth
            self.sent = self.got = 0

        def ready(self, got):
            more = []
            while self.sent < len(self.order) and self.sent < got + self.depth:
                section, hop = self.order[self.sent]
                if hop and (section, hop - 1) not in self.order[:got]:
                    break
                more.append((section, hop))
                self.sent += 1
            return more

        def begin(self):
            for section, hop in self.ready(self.got):
                for way in range(2):
                    section.send(way, hop)

        def extend(self, order):
            self.order += order
            self.begin()

        def advance(self, upto=None):
            upto = self.got + 1 if upto is None else upto
            while self.got < min(upto, len(self.order)):
                section, hop = self.order[self.got]
                following = self.ready(self.got + 1)
                now = [pair for pair in following if pair[1]]
                shared = []
                for way in range(2):
                    shared.append((way, hop, *section.receive(way, hop)))
                    for later, later_hop in now:
                        later.send(way, later_hop)
                for one in shared:
                    section.share(*one)
                for later, later_hop in following:
                    for way in range(2):
                        if not later_hop:
                            later.send(way, later_hop)
                section.settle(hop - 1)
                self.got += 1

        def through(self, section):
            return self.order.index((section, 3)) + 1

    class Mirror:
        def __init__(self, name, mine, buf):
            self.name, self.mine, self.buf = name, mine, buf

        def block(self, slot):
            return self.buf.at[slot, 1]

        def take(self, slot, what):
            block = self.block(slot)
            arrived(block, (self.mine, "mate", what))
            push(block, block, to_sib, (self.name, "sib", what))

        def start(self):
            self.take(row, "own")

        def step(self, j):
            for way in range(2):
                self.take(away(row, way, j + 1), (way, j))
            self.settle(j - 1)

        def last(self):
            self.take(away(row, 0, 4), "far")
            self.settle(2)

        def settle(self, j):
            if j < 0:
                arrived(self.block(sib), (self.name, "sib", "own"))
            else:
                for way in range(2):
                    arrived(self.block(away(sib, way, j + 1)), (self.name, "sib", (way, j)))

        def done(self):
            arrived(self.block(away(sib, 0, 4)), (self.name, "sib", "far"))

    def faces_of(rows, i):
        inside = lax.rem(i, 8)
        lanes = pl.ds(pl.multiple_of(z * 128, 128), 128)
        whole = jnp.sum(
            jnp.where(iota((8, ORDER), 0) == inside, rows[...], 0), axis=0, keepdims=True
        )
        chunk = jnp.sum(
            jnp.where(iota((8, 128), 0) == inside, rows[:, lanes], 0), axis=0, keepdims=True
        )
        local = jnp.where(core == 0, chunk[:, :64], chunk[:, 64:])
        return whole, local

    def select(child, own_index, pair_index):
        own_faces, local = faces_of(child_rows, own_index)
        paired, _ = faces_of(child_rows, pair_index)
        hot = build_selectors(own_faces, paired, local, face_hot, outer_hot)
        loads[2 - child].wait()
        stack = select_rows([maps[child, part] for part in range(2)], hot)
        face = joined(dot_nt(stack, face_hot[...]))
        outer = jnp.concatenate(
            [dot_nt(stack[:, 256 * t : 256 * t + 256], outer_hot[t]) for t in range(4)], axis=1
        )
        return face, joined(outer)

    loads[0].wait()
    face, outer = select(1, first + 1 + par, first + 3 - 3 * par)
    for part in range(2):
        out_ss[part] = face[part][:32]
        out_xs[part] = face[part][32:]
        out_xx[part] = outer[part][32:]
        halves = [outer[part][:32, :256], outer[part][:32, 256:]]
        out_sx[0, part] = pick(par, halves[1], halves[0])
        out_sx[1, part] = pick(par, halves[0], halves[1])
    pl.semaphore_wait(barrier, 4)
    push(out_ss, ss1.at[par, row], to_mate, "ss1")

    face, outer = select(0, first + 3 * par, first + 2 - par)
    for part in range(2):
        ss1[par, row, part] = face[part][:32]
        xs1[par, part] = face[part][32:]
        xx1[par, part] = outer[part][32:]
        halves = [outer[part][:32, :256], outer[part][:32, 256:]]
        sx1a[row, par, part] = pick(par, halves[0], halves[1])
        sx1b[par, row, part] = pick(par, halves[1], halves[0])
    ssm = Section("ssm1", ss1.at[par])
    sso = Section("sso1", ss1.at[1 - par], source=(ss1.at[1 - par, row], "ss1"))
    xa = Section("sxa1", sx1a, source=(sx1a.at[row, 1 - par], "mate sxa1"))
    mb = Section("sxm1", sx1b.at[par])
    ob = Section("sxo1", sx1b.at[1 - par], source=(sx1b.at[1 - par, row], "mate sxb1"))
    flow = Flow(order_parent(ssm, sso, xa, mb, ob), 2)
    flow.begin()
    push(out_sx.at[0], sx1a.at[row, par], to_mate, "mate sxa1")
    flow.depth = DEPTHS[0]
    flow.begin()

    def horner(ss, xs, more):
        convert(lambda k, part: ss[1, k, part], wss.at[1])
        u = [xs[0, part] for part in range(2)]
        lead = complex_product(u, wss.at[1])
        base = [jnp.concatenate([lead[part], -xs[1, part]], axis=0) for part in range(2)]
        more()
        convert(lambda k, part: ss[0, k, part], wss.at[0])
        w = base
        for term in range(3):
            t = complex_product(w, wss.at[0])
            more()
            t = complex_product(t, wss.at[1])
            w = [base[part] + t[part] for part in range(2)]
            more()
        t = complex_product(w, wss.at[0])
        t = [jnp.concatenate([t[part][:32] + u[part], t[part][32:]], axis=0) for part in range(2)]
        return w, t

    rank, place = iota((256, 256), 0), iota((256, 256), 1)
    inside = jnp.where(rank < 128, rank, rank - 128)
    spot = 32 * lax.div(inside, 16) + lax.rem(inside, 16) + jnp.where(rank < 128, 0, 16)
    place_hot[...] = one_hot(spot == place)

    def finish(w, t, wx, xx):
        alpha, beta = complex_product(w, wx.at[0]), complex_product(t, wx.at[1])
        tiles = []
        for part in range(2):
            left = weave(xx[0][part] + alpha[part][:32], alpha[part][32:])
            right = weave(-beta[part][:32], xx[1][part] - beta[part][32:])
            tiles.append((left, right))
        columns = []
        for tile in range(2):
            cols = slice(128 * tile, 128 * tile + 128)
            packed = jnp.concatenate(
                [jnp.concatenate([left[:, cols], right[:, cols]], axis=1) for left, right in tiles],
                axis=0,
            )
            hi, lo = split(packed)
            spread = dot(jnp.concatenate([hi, lo], axis=0), place_hot[...])
            columns.append(spread[:128] + spread[128:])
        both = jnp.concatenate(columns, axis=1)
        return [both[:64], both[64:]]

    loads[3].wait()
    own, loc = faces_of(parent_rows, box)
    pair, _ = faces_of(parent_rows, mate)
    hot2 = build_selectors(own, pair, loc, face_hot2, outer_hot2)
    flow.advance(2)
    push(out_sx.at[1], sx1b.at[par, row], to_mate, "mate sxb1")
    flow.advance(3)
    push(out_xs, xs1.at[par], to_mate, "xs1")
    push(out_xx, xx1.at[par], to_mate, "xx1")
    flow.advance(max(flow.through(ssm), flow.through(sso)))
    arrived(xs1.at[1 - par], "xs1")
    arrived(xx1.at[1 - par], "xx1")
    ssm.done()
    sso.done()
    w, t = horner(ss1, xs1, lambda: flow.advance(min(flow.got + 1, flow.through(xa))))

    ssi, ssr = Section("ssi2", ss2.at[par], part=1, forward=True), Section("ssr2", ss2.at[par], part=0)
    sso = Section("sso2", ss2.at[1 - par], part=0, source=(ss2.at[1 - par, row, 0], "ss2"))
    mirror = Mirror("mir2", "ssi2", ss2.at[1 - par])
    sxm = Section("sxm2", sx2.at[par])
    sxo = Section("sxo2", sx2.at[1 - par], source=(sx2.at[1 - par, row], "sx2"))
    face = jnp.zeros((256, 512), F32)
    for h in range(2):
        side = par if h == 0 else 1 - par
        lanes = pl.ds(pl.multiple_of(256 * side, 256), 256)
        if h == 0:
            flow.advance(flow.through(xa))
            xa.done()
        else:
            flow.advance(max(flow.through(mb), flow.through(ob)) + 1)
            mb.done()
            ob.done()
        for role in range(2):
            if h == 0:
                convert(lambda k, part: sx1a[k, role, part], wsx.at[h, role])
            else:
                convert(lambda k, part: sx1b[role, k, part], wsx.at[h, role])
        xx = [[xx1[role, part, :, lanes] for part in range(2)] for role in range(2)]
        merged = finish(w, t, wsx.at[h], xx)
        wide = pl.ds(pl.multiple_of(512 * side, 512), 512)
        for part in range(2):
            parent_ref[part, :, wide] = merged[part]
        stack = select_rows(merged, hot2)
        outer = joined(
            jnp.concatenate(
                [dot_nt(stack[:, 256 * i : 256 * i + 256], outer_hot2[2 * side + i]) for i in range(2)],
                axis=1,
            )
        )
        if h == 0:
            for part in range(2):
                sx2[par, row, part] = outer[part][:32]
                xx2[par, part] = outer[part][32:]
            flow.extend([(sxm, 0), (sxm, 1)])
        face = face + dot_nt(stack, face_hot2[:, wide])
    face = joined(face)
    for part in range(2):
        ss2[par, row, part] = face[part][:32]
        xs2[par, part] = face[part][32:]
    real = ss2.at[par, row, 0]
    push(real, real, to_mate, "ss2")
    flow.depth = DEPTHS[1]
    flow.extend(order_grand(ssi, ssr, sso, sxm, sxo))
    for part in range(2):
        out_sx2[part] = outer[part][:32]
        out_xx2[part] = outer[part][32:]
    push(out_sx2, sx2.at[par, row], to_mate, "sx2")
    store = pltpu.make_async_copy(parent_ref, parent_out.at[:, 0], local_sem.at[4])
    store.start()
    drain(30)
    at = [flow.order.index((ssi, hop)) + 1 for hop in range(4)]
    flow.advance(at[0])
    push(xs2.at[par], xs2.at[par], to_mate, "xs2")
    mirror.start()
    flow.advance(at[1])
    mirror.step(0)
    push(out_xx2, xx2.at[par], to_mate, "xx2")
    flow.advance(at[2])
    mirror.step(1)
    flow.advance(max(flow.through(ssi), flow.through(ssr), flow.through(sso)))
    mirror.step(2)
    mirror.last()
    arrived(xs2.at[1 - par], "xs2")
    arrived(xx2.at[1 - par], "xx2")
    flow.advance()
    ssi.done()
    ssr.done()
    sso.done()
    mirror.done()
    w, t = horner(ss2, xs2, flow.advance)
    drain(16)
    flow.advance(len(flow.order))
    sxm.done()
    sxo.done()
    for role in range(2):
        convert(lambda k, part: sx2[role, k, part], wsx2.at[role])
    xx = [[xx2[role, part] for part in range(2)] for role in range(2)]
    merged = finish(w, t, wsx2, xx)
    for part in range(2):
        grand_ref[part] = merged[part]

    store.wait()
    drain(0)
    assert len(ids) <= TOTAL


def per_device(child_maps, child_faces, parent_faces):
    def vmem(*shape, dtype=F32):
        return pltpu.VMEM(shape, dtype)

    whole = pl.BlockSpec(memory_space=pltpu.VMEM)
    placed = pl.BlockSpec(memory_space=pltpu.HBM)
    return pl.pallas_call(
        kernel,
        out_shape=(
            jax.ShapeDtypeStruct((2, 1, 64, ORDER), F32),
            jax.ShapeDtypeStruct((2, 64, SHARED), F32),
        ),
        in_specs=[placed] * 3,
        out_specs=(placed, whole),
        scratch_shapes=[
            vmem(2, 2, 64, ORDER), pltpu.VMEM((8, ORDER), jnp.int32), pltpu.VMEM((8, ORDER), jnp.int32),
            vmem(2, 64, ORDER),
            vmem(2, RING, 2, 32, 512), vmem(RING, 2, 2, 32, 256), vmem(2, RING, 2, 32, 256), vmem(2, 2, 32, 512), vmem(2, 2, 32, 512),
            vmem(2, RING, 2, 32, 512), vmem(2, RING, 2, 32, 256), vmem(2, 2, 32, 512), vmem(2, 2, 32, 256),
            vmem(2, 32, 512), vmem(2, 2, 32, 256), vmem(2, 32, 512), vmem(2, 32, 512),
            vmem(2, 32, 256), vmem(2, 32, 256),
            vmem(512, 1024, dtype=BF16), vmem(4, 128, 256, dtype=BF16),
            vmem(512, 1024, dtype=BF16), vmem(4, 128, 256, dtype=BF16),
            vmem(256, 256, dtype=BF16),
            vmem(2, 2, 2, 512, 512, dtype=BF16),
            vmem(2, 2, 2, 2, 512, 256, dtype=BF16),
            vmem(2, 2, 2, 512, 256, dtype=BF16),
            pltpu.SemaphoreType.DMA((TOTAL,)),
            pltpu.SemaphoreType.DMA((TOTAL,)),
            pltpu.SemaphoreType.DMA((5,)),
        ],
        compiler_params=pltpu.CompilerParams(
            collective_id=0, has_side_effects=True, vmem_limit_bytes=58 * 1024 * 1024
        ),
    )(child_maps, child_faces, parent_faces)


def solution(mesh):
    placed = (P(None, "box", "row", None), P(), P())
    return jax.shard_map(
        per_device,
        mesh=mesh,
        in_specs=placed,
        out_specs=(P(None, "box", "row", None), P(None, "row", "box")),
        check_vma=False,
    )
```

```python
import functools

import jax
import jax.numpy as jnp
from jax import lax
from jax.experimental import pallas as pl
from jax.experimental.pallas import tpu as pltpu
from jax.sharding import PartitionSpec as P

MESH = pl.DeviceIdType.MESH
F32 = jnp.float32
BF16 = jnp.bfloat16
ORDER = 1024
SHARED = 512
RING = 16
TOTAL = 208
DEPTHS = (4, 4)


def order_parent(ssm, sso, xa, mb, ob):
    return [
        (ssm, 0), (mb, 0), (sso, 0), (ssm, 1), (xa, 0), (sso, 1), (ssm, 2), (sso, 2), (xa, 1),
        (ssm, 3), (sso, 3), (ob, 0), (mb, 1), (xa, 2), (ob, 1), (mb, 2), (xa, 3), (ob, 2),
        (mb, 3), (ob, 3),
    ]


def order_grand(ssi, ssr, sso, sxm, sxo):
    return [
        (ssi, 0), (ssr, 0), (sso, 0), (ssi, 1), (ssr, 1), (sso, 1), (sxm, 2), (ssi, 2), (ssr, 2),
        (sso, 2), (sxo, 0), (ssi, 3), (ssr, 3), (sso, 3), (sxo, 1), (sxm, 3), (sxo, 2), (sxo, 3),
    ]


def dot(a, b):
    return jnp.dot(a, b, preferred_element_type=F32)


def dot_nt(a, b):
    return lax.dot_general(a, b, (((1,), (1,)), ((), ())), preferred_element_type=F32)


def split(x):
    hi = x.astype(BF16)
    return hi, (x - hi.astype(F32)).astype(BF16)


def iota(shape, dim):
    return lax.broadcasted_iota(jnp.int32, shape, dim)


def one_hot(mask):
    return jnp.where(mask, 1.0, 0.0).astype(BF16)


def prefix_counts(rows):
    width = rows.shape[1]
    lower = one_hot(iota((width, width), 0) < iota((width, width), 1))
    return dot(jnp.where(rows < 0, 1.0, 0.0).astype(BF16), lower).astype(jnp.int32)


def chunked(faces):
    return jnp.concatenate([faces[:, 256 * t : 256 * t + 256] for t in range(4)], axis=0)


def build_selectors(own, other, local, face_ref, outer_ref):
    rows = jnp.concatenate([chunked(own), chunked(other)], axis=0)
    counts = prefix_counts(rows)
    lane = iota((1, 256), 1)
    slot = iota((128, 256), 0)
    own_value = own.astype(F32)
    for t in range(4):
        outer_rank = jnp.where(rows[t : t + 1] < 0, counts[t : t + 1], -1)
        outer_ref[t] = one_hot(outer_rank == slot)
        face_row = rows[4 + t : 5 + t]
        shared_rank = jnp.where(face_row < 0, -1, lane - counts[4 + t : 5 + t])
        wanted = jnp.sum(
            jnp.where(shared_rank == slot, face_row.astype(F32), 0.0), axis=1, keepdims=True
        )
        face_ref[128 * t : 128 * t + 128, :] = one_hot(own_value == wanted)
    count = prefix_counts(jnp.broadcast_to(local, (8, 64)))[0:1]
    target = jnp.where(local < 0, 32 + count, iota((1, 64), 1) - count)
    return one_hot(target == iota((64, 64), 0))


def select_rows(parts, row_hot):
    stack = []
    for value in parts:
        for piece in split(value):
            stack.append(dot(row_hot, piece).astype(BF16))
    return jnp.concatenate(stack, axis=0)


def joined(stack):
    return [stack[0:64] + stack[64:128], stack[128:192] + stack[192:256]]


def pick(par, former, latter):
    return jnp.where(par == 0, former, latter)


def complex_product(x, w):
    m = x[0].shape[0]
    hi, lo = split(jnp.concatenate(x, axis=0))
    both = jnp.concatenate([hi, lo], axis=0)
    sums = []
    for part in range(2):
        main = dot(both, w[0, part])
        sums.append(main[: 2 * m] + main[2 * m :] + dot(hi, w[1, part]))
    by_real, by_imag = sums
    return [by_real[:m] - by_imag[m:], by_imag[:m] + by_real[m:]]


def convert(fetch, pieces):
    @pl.loop(0, RING)
    def _(k):
        rows = pl.ds(pl.multiple_of(k * 32, 32), 32)
        for part in range(2):
            hi, lo = split(fetch(k, part))
            pieces[0, part, rows, :] = hi
            pieces[1, part, rows, :] = lo


def weave(alpha, beta):
    return jnp.concatenate([alpha[0:16], beta[0:16], alpha[16:32], beta[16:32]], axis=0)


def kernel(
    maps_ref, child_faces_ref, parent_faces_ref, parent_out, grand_ref,
    maps, child_rows, parent_rows, parent_ref,
    ss1, sx1a, sx1b, xs1, xx1, ss2, sx2, xs2, xx2, out_ss, out_sx, out_xs, out_xx, out_sx2, out_xx2,
    face_hot, outer_hot, face_hot2, outer_hot2, place_hot, wss, wsx, wsx2, send, recv, local_sem,
):
    box, row = lax.axis_index("box"), lax.axis_index("row")
    par = lax.rem(box, 2)
    mate = box + 1 - 2 * par
    core = lax.rem(row, 2)
    z = lax.div(row, 2)
    sib = row + 1 - 2 * core
    up, down = lax.rem(row + 2, RING), lax.rem(row + RING - 2, RING)
    to_up, to_down, to_sib, to_mate = (box, up), (box, down), (box, sib), (mate, row)

    barrier = pltpu.get_barrier_semaphore()
    for target in (to_up, to_down, to_sib, to_mate):
        pl.semaphore_signal(barrier, inc=1, device_id=target, device_id_type=MESH)

    first = 2 * (box - par)

    def group(i):
        return pl.ds(pl.multiple_of(8 * lax.div(i, 8), 8), 8)

    loads = [
        pltpu.make_async_copy(child_faces_ref.at[group(first)], child_rows, local_sem.at[0]),
        pltpu.make_async_copy(maps_ref.at[:, 1 - par], maps.at[1], local_sem.at[1]),
        pltpu.make_async_copy(maps_ref.at[:, par], maps.at[0], local_sem.at[2]),
        pltpu.make_async_copy(parent_faces_ref.at[group(box)], parent_rows, local_sem.at[3]),
    ]
    for c in loads:
        c.start()

    ids = {}
    pending = []

    def copy(src, dst, target, key):
        k = ids.setdefault(key, len(ids))
        return pltpu.make_async_remote_copy(
            src_ref=src, dst_ref=dst, send_sem=send.at[k], recv_sem=recv.at[k],
            device_id=target, device_id_type=MESH,
        )

    def push(src, dst, target, key):
        c = copy(src, dst, target, key)
        c.start()
        pending.append(c)

    def drain(spare):
        while len(pending) > spare:
            pending.pop(0).wait_send()

    def arrived(dst, key):
        copy(dst, dst, to_mate, key).wait_recv()

    def away(base, way, hops):
        return lax.rem(base + 2 * RING + (2 if way else -2) * hops, RING)

    class Section:
        settled = -1

        def __init__(self, name, buf, part=None, forward=False, source=None):
            self.name, self.buf, self.part, self.forward, self.source = name, buf, part, forward, source

        def block(self, slot):
            return self.buf.at[slot] if self.part is None else self.buf.at[slot, self.part]

        def piece(self, base, way, hop):
            slot = away(base, way, hop)
            if hop < 3:
                return self.block(slot)
            if self.part is not None:
                return self.buf.at[slot, self.part, pl.ds(16 * way, 16)]
            return self.buf.at[slot, way]

        def to_mate(self, slot, what):
            if self.forward:
                block = self.block(slot)
                push(block, block, to_mate, (self.name, "mate", what))

        def send(self, way, hop):
            if hop == 0 and way == 0 and self.source is not None:
                arrived(*self.source)
            piece = self.piece(row, way, hop)
            push(piece, piece, to_down if way else to_up, (self.name, way, hop))
            if hop == 0 and way == 1:
                own = self.block(row)
                push(own, own, to_sib, (self.name, "sib", "own"))
                self.to_mate(row, "own")

        def receive(self, way, hop):
            slot = away(row, way, hop + 1)
            if hop < 3:
                piece = self.block(slot)
            else:
                piece = self.piece(away(row, way, 1), way, hop)
            arrived(piece, (self.name, way, hop))
            return slot, piece

        def share(self, way, hop, slot, piece):
            push(piece, piece, to_sib, (self.name, "sib", way, hop))
            if hop < 3:
                self.to_mate(slot, (way, hop))
            elif way == 1:
                self.to_mate(slot, "far")

        def settle(self, hop):
            while self.settled <= hop:
                if self.settled < 0:
                    arrived(self.block(sib), (self.name, "sib", "own"))
                else:
                    for way in range(2):
                        if self.settled < 3:
                            piece = self.block(away(sib, way, self.settled + 1))
                        else:
                            piece = self.piece(away(sib, way, 1), way, 3)
                        arrived(piece, (self.name, "sib", way, self.settled))
                self.settled += 1

        def done(self):
            self.settle(3)

    class Flow:
        def __init__(self, order, depth):
            self.order, self.depth = order, depth
            self.sent = self.got = 0

        def ready(self, got):
            more = []
            while self.sent < len(self.order) and self.sent < got + self.depth:
                section, hop = self.order[self.sent]
                if hop and (section, hop - 1) not in self.order[:got]:
                    break
                more.append((section, hop))
                self.sent += 1
            return more

        def begin(self):
            for section, hop in self.ready(self.got):
                for way in range(2):
                    section.send(way, hop)

        def extend(self, order):
            self.order += order
            self.begin()

        def advance(self, upto=None):
            upto = self.got + 1 if upto is None else upto
            while self.got < min(upto, len(self.order)):
                section, hop = self.order[self.got]
                following = self.ready(self.got + 1)
                now = [pair for pair in following if pair[1]]
                shared = []
                for way in range(2):
                    shared.append((way, hop, *section.receive(way, hop)))
                    for later, later_hop in now:
                        later.send(way, later_hop)
                for one in shared:
                    section.share(*one)
                for later, later_hop in following:
                    for way in range(2):
                        if not later_hop:
                            later.send(way, later_hop)
                section.settle(hop - 1)
                self.got += 1

        def through(self, section):
            return self.order.index((section, 3)) + 1

    class Mirror:
        def __init__(self, name, mine, buf):
            self.name, self.mine, self.buf = name, mine, buf

        def block(self, slot):
            return self.buf.at[slot, 1]

        def take(self, slot, what):
            block = self.block(slot)
            arrived(block, (self.mine, "mate", what))
            push(block, block, to_sib, (self.name, "sib", what))

        def start(self):
            self.take(row, "own")

        def step(self, j):
            for way in range(2):
                self.take(away(row, way, j + 1), (way, j))
            self.settle(j - 1)

        def last(self):
            self.take(away(row, 0, 4), "far")
            self.settle(2)

        def settle(self, j):
            if j < 0:
                arrived(self.block(sib), (self.name, "sib", "own"))
            else:
                for way in range(2):
                    arrived(self.block(away(sib, way, j + 1)), (self.name, "sib", (way, j)))

        def done(self):
            arrived(self.block(away(sib, 0, 4)), (self.name, "sib", "far"))

    def faces_of(rows, i):
        inside = lax.rem(i, 8)
        lanes = pl.ds(pl.multiple_of(z * 128, 128), 128)
        whole = jnp.sum(
            jnp.where(iota((8, ORDER), 0) == inside, rows[...], 0), axis=0, keepdims=True
        )
        chunk = jnp.sum(
            jnp.where(iota((8, 128), 0) == inside, rows[:, lanes], 0), axis=0, keepdims=True
        )
        local = jnp.where(core == 0, chunk[:, :64], chunk[:, 64:])
        return whole, local

    def select(child, own_index, pair_index):
        own_faces, local = faces_of(child_rows, own_index)
        paired, _ = faces_of(child_rows, pair_index)
        hot = build_selectors(own_faces, paired, local, face_hot, outer_hot)
        loads[2 - child].wait()
        stack = select_rows([maps[child, part] for part in range(2)], hot)
        face = joined(dot_nt(stack, face_hot[...]))
        outer = jnp.concatenate(
            [dot_nt(stack[:, 256 * t : 256 * t + 256], outer_hot[t]) for t in range(4)], axis=1
        )
        return face, joined(outer)

    loads[0].wait()
    face, outer = select(1, first + 1 + par, first + 3 - 3 * par)
    for part in range(2):
        out_ss[part] = face[part][:32]
        out_xs[part] = face[part][32:]
        out_xx[part] = outer[part][32:]
        halves = [outer[part][:32, :256], outer[part][:32, 256:]]
        out_sx[0, part] = pick(par, halves[1], halves[0])
        out_sx[1, part] = pick(par, halves[0], halves[1])
    pl.semaphore_wait(barrier, 4)
    push(out_ss, ss1.at[par, row], to_mate, "ss1")

    face, outer = select(0, first + 3 * par, first + 2 - par)
    for part in range(2):
        ss1[par, row, part] = face[part][:32]
        xs1[par, part] = face[part][32:]
        xx1[par, part] = outer[part][32:]
        halves = [outer[part][:32, :256], outer[part][:32, 256:]]
        sx1a[row, par, part] = pick(par, halves[0], halves[1])
        sx1b[par, row, part] = pick(par, halves[1], halves[0])
    ssm = Section("ssm1", ss1.at[par])
    sso = Section("sso1", ss1.at[1 - par], source=(ss1.at[1 - par, row], "ss1"))
    xa = Section("sxa1", sx1a, source=(sx1a.at[row, 1 - par], "mate sxa1"))
    mb = Section("sxm1", sx1b.at[par])
    ob = Section("sxo1", sx1b.at[1 - par], source=(sx1b.at[1 - par, row], "mate sxb1"))
    flow = Flow(order_parent(ssm, sso, xa, mb, ob), 2)
    flow.begin()
    push(out_sx.at[0], sx1a.at[row, par], to_mate, "mate sxa1")
    flow.depth = DEPTHS[0]
    flow.begin()

    def horner(ss, xs, more):
        convert(lambda k, part: ss[1, k, part], wss.at[1])
        u = [xs[0, part] for part in range(2)]
        lead = complex_product(u, wss.at[1])
        base = [jnp.concatenate([lead[part], -xs[1, part]], axis=0) for part in range(2)]
        more()
        convert(lambda k, part: ss[0, k, part], wss.at[0])
        w = base
        for term in range(3):
            t = complex_product(w, wss.at[0])
            more()
            t = complex_product(t, wss.at[1])
            w = [base[part] + t[part] for part in range(2)]
            more()
        t = complex_product(w, wss.at[0])
        t = [jnp.concatenate([t[part][:32] + u[part], t[part][32:]], axis=0) for part in range(2)]
        return w, t

    rank, place = iota((256, 256), 0), iota((256, 256), 1)
    inside = jnp.where(rank < 128, rank, rank - 128)
    spot = 32 * lax.div(inside, 16) + lax.rem(inside, 16) + jnp.where(rank < 128, 0, 16)
    place_hot[...] = one_hot(spot == place)

    def finish(alpha, beta, xx):
        tiles = []
        for part in range(2):
            left = weave(xx[0][part] + alpha[part][:32], alpha[part][32:])
            right = weave(-beta[part][:32], xx[1][part] - beta[part][32:])
            tiles.append((left, right))
        columns = []
        for tile in range(2):
            cols = slice(128 * tile, 128 * tile + 128)
            packed = jnp.concatenate(
                [jnp.concatenate([left[:, cols], right[:, cols]], axis=1) for left, right in tiles],
                axis=0,
            )
            hi, lo = split(packed)
            spread = dot(jnp.concatenate([hi, lo], axis=0), place_hot[...])
            columns.append(spread[:128] + spread[128:])
        both = jnp.concatenate(columns, axis=1)
        return [both[:64], both[64:]]

    loads[3].wait()
    own, loc = faces_of(parent_rows, box)
    pair, _ = faces_of(parent_rows, mate)
    hot2 = build_selectors(own, pair, loc, face_hot2, outer_hot2)
    flow.advance(2)
    push(out_sx.at[1], sx1b.at[par, row], to_mate, "mate sxb1")
    flow.advance(3)
    push(out_xs, xs1.at[par], to_mate, "xs1")
    push(out_xx, xx1.at[par], to_mate, "xx1")
    flow.advance(max(flow.through(ssm), flow.through(sso)))
    arrived(xs1.at[1 - par], "xs1")
    arrived(xx1.at[1 - par], "xx1")
    ssm.done()
    sso.done()
    w, t = horner(ss1, xs1, lambda: flow.advance(min(flow.got + 1, flow.through(xa))))

    ssi, ssr = Section("ssi2", ss2.at[par], part=1, forward=True), Section("ssr2", ss2.at[par], part=0)
    sso = Section("sso2", ss2.at[1 - par], part=0, source=(ss2.at[1 - par, row, 0], "ss2"))
    mirror = Mirror("mir2", "ssi2", ss2.at[1 - par])
    sxm = Section("sxm2", sx2.at[par])
    sxo = Section("sxo2", sx2.at[1 - par], source=(sx2.at[1 - par, row], "sx2"))
    face = jnp.zeros((256, 512), F32)
    for h in range(2):
        side = par if h == 0 else 1 - par
        lanes = pl.ds(pl.multiple_of(256 * side, 256), 256)
        if h == 0:
            flow.advance(flow.through(xa))
            xa.done()
        else:
            flow.advance(max(flow.through(mb), flow.through(ob)) + 1)
            mb.done()
            ob.done()
        for role in range(2):
            if h == 0:
                convert(lambda k, part: sx1a[k, role, part], wsx.at[h, role])
            else:
                convert(lambda k, part: sx1b[role, k, part], wsx.at[h, role])
        xx = [[xx1[role, part, :, lanes] for part in range(2)] for role in range(2)]
        alpha, beta = complex_product(w, wsx.at[h, 0]), complex_product(t, wsx.at[h, 1])
        merged = finish(alpha, beta, xx)
        wide = pl.ds(pl.multiple_of(512 * side, 512), 512)
        for part in range(2):
            parent_ref[part, :, wide] = merged[part]
        stack = select_rows(merged, hot2)
        outer = joined(
            jnp.concatenate(
                [dot_nt(stack[:, 256 * i : 256 * i + 256], outer_hot2[2 * side + i]) for i in range(2)],
                axis=1,
            )
        )
        if h == 0:
            for part in range(2):
                sx2[par, row, part] = outer[part][:32]
                xx2[par, part] = outer[part][32:]
            flow.extend([(sxm, 0), (sxm, 1)])
        face = face + dot_nt(stack, face_hot2[:, wide])
    face = joined(face)
    for part in range(2):
        ss2[par, row, part] = face[part][:32]
        xs2[par, part] = face[part][32:]
    real = ss2.at[par, row, 0]
    push(real, real, to_mate, "ss2")
    flow.depth = DEPTHS[1]
    flow.extend(order_grand(ssi, ssr, sso, sxm, sxo))
    for part in range(2):
        out_sx2[part] = outer[part][:32]
        out_xx2[part] = outer[part][32:]
    push(out_sx2, sx2.at[par, row], to_mate, "sx2")
    store = pltpu.make_async_copy(parent_ref, parent_out.at[:, 0], local_sem.at[4])
    store.start()
    drain(30)
    at = [flow.order.index((ssi, hop)) + 1 for hop in range(4)]
    flow.advance(at[0])
    push(xs2.at[par], xs2.at[par], to_mate, "xs2")
    mirror.start()
    flow.advance(at[1])
    mirror.step(0)
    push(out_xx2, xx2.at[par], to_mate, "xx2")
    flow.advance(at[2])
    mirror.step(1)
    flow.advance(max(flow.through(ssi), flow.through(ssr), flow.through(sso)))
    mirror.step(2)
    mirror.last()
    arrived(xs2.at[1 - par], "xs2")
    arrived(xx2.at[1 - par], "xx2")
    flow.advance()
    ssi.done()
    ssr.done()
    sso.done()
    mirror.done()
    w, t = horner(ss2, xs2, flow.advance)
    drain(16)
    products = []
    for section, role, rows in ((sxm, par, (w, t)), (sxo, 1 - par, (t, w))):
        flow.advance(flow.through(section))
        section.done()
        convert(lambda k, part: sx2[role, k, part], wsx2.at[role])
        picked = [pick(par, rows[0][part], rows[1][part]) for part in range(2)]
        products.append(complex_product(picked, wsx2.at[role]))
    own, far = products
    alpha = [pick(par, own[part], far[part]) for part in range(2)]
    beta = [pick(par, far[part], own[part]) for part in range(2)]
    xx = [[xx2[role, part] for part in range(2)] for role in range(2)]
    merged = finish(alpha, beta, xx)
    for part in range(2):
        grand_ref[part] = merged[part]

    store.wait()
    drain(0)
    assert len(ids) <= TOTAL


def per_device(child_maps, child_faces, parent_faces):
    def vmem(*shape, dtype=F32):
        return pltpu.VMEM(shape, dtype)

    whole = pl.BlockSpec(memory_space=pltpu.VMEM)
    placed = pl.BlockSpec(memory_space=pltpu.HBM)
    return pl.pallas_call(
        kernel,
        out_shape=(
            jax.ShapeDtypeStruct((2, 1, 64, ORDER), F32),
            jax.ShapeDtypeStruct((2, 64, SHARED), F32),
        ),
        in_specs=[placed] * 3,
        out_specs=(placed, whole),
        scratch_shapes=[
            vmem(2, 2, 64, ORDER), pltpu.VMEM((8, ORDER), jnp.int32), pltpu.VMEM((8, ORDER), jnp.int32),
            vmem(2, 64, ORDER),
            vmem(2, RING, 2, 32, 512), vmem(RING, 2, 2, 32, 256), vmem(2, RING, 2, 32, 256), vmem(2, 2, 32, 512), vmem(2, 2, 32, 512),
            vmem(2, RING, 2, 32, 512), vmem(2, RING, 2, 32, 256), vmem(2, 2, 32, 512), vmem(2, 2, 32, 256),
            vmem(2, 32, 512), vmem(2, 2, 32, 256), vmem(2, 32, 512), vmem(2, 32, 512),
            vmem(2, 32, 256), vmem(2, 32, 256),
            vmem(512, 1024, dtype=BF16), vmem(4, 128, 256, dtype=BF16),
            vmem(512, 1024, dtype=BF16), vmem(4, 128, 256, dtype=BF16),
            vmem(256, 256, dtype=BF16),
            vmem(2, 2, 2, 512, 512, dtype=BF16),
            vmem(2, 2, 2, 2, 512, 256, dtype=BF16),
            vmem(2, 2, 2, 512, 256, dtype=BF16),
            pltpu.SemaphoreType.DMA((TOTAL,)),
            pltpu.SemaphoreType.DMA((TOTAL,)),
            pltpu.SemaphoreType.DMA((5,)),
        ],
        compiler_params=pltpu.CompilerParams(
            collective_id=0, has_side_effects=True, vmem_limit_bytes=58 * 1024 * 1024
        ),
    )(child_maps, child_faces, parent_faces)


def solution(mesh):
    placed = (P(None, "box", "row", None), P(), P())
    return jax.shard_map(
        per_device,
        mesh=mesh,
        in_specs=placed,
        out_specs=(P(None, "box", "row", None), P(None, "row", "box")),
        check_vma=False,
    )
```

```python
import functools

import jax
import jax.numpy as jnp
from jax import lax
from jax.experimental import pallas as pl
from jax.experimental.pallas import tpu as pltpu
from jax.sharding import PartitionSpec as P

MESH = pl.DeviceIdType.MESH
F32 = jnp.float32
BF16 = jnp.bfloat16
ORDER = 1024
SHARED = 512
RING = 16
TOTAL = 208
DEPTHS = (4, 4)


def order_parent(ssm, sso, xa, mb, ob):
    return [
        (ssm, 0), (mb, 0), (sso, 0), (ssm, 1), (xa, 0), (sso, 1), (ssm, 2), (sso, 2), (xa, 1),
        (ssm, 3), (sso, 3), (ob, 0), (mb, 1), (xa, 2), (ob, 1), (mb, 2), (xa, 3), (ob, 2),
        (mb, 3), (ob, 3),
    ]


def order_grand(ssi, ssr, sso, sxm, sxo):
    return [
        (ssi, 0), (ssr, 0), (sso, 0), (ssi, 1), (ssr, 1), (sso, 1), (sxm, 2), (ssi, 2), (ssr, 2),
        (sso, 2), (sxo, 0), (ssi, 3), (ssr, 3), (sso, 3), (sxo, 1), (sxm, 3), (sxo, 2), (sxo, 3),
    ]


def dot(a, b):
    return jnp.dot(a, b, preferred_element_type=F32)


def dot_nt(a, b):
    return lax.dot_general(a, b, (((1,), (1,)), ((), ())), preferred_element_type=F32)


def split(x):
    hi = x.astype(BF16)
    return hi, (x - hi.astype(F32)).astype(BF16)


def iota(shape, dim):
    return lax.broadcasted_iota(jnp.int32, shape, dim)


def one_hot(mask):
    return jnp.where(mask, 1.0, 0.0).astype(BF16)


def prefix_counts(rows):
    width = rows.shape[1]
    lower = one_hot(iota((width, width), 0) < iota((width, width), 1))
    return dot(jnp.where(rows < 0, 1.0, 0.0).astype(BF16), lower).astype(jnp.int32)


def chunked(faces):
    return jnp.concatenate([faces[:, 256 * t : 256 * t + 256] for t in range(4)], axis=0)


def build_selectors(own, other, local, face_ref, outer_ref):
    rows = jnp.concatenate([chunked(own), chunked(other)], axis=0)
    counts = prefix_counts(rows)
    lane = iota((1, 256), 1)
    slot = iota((128, 256), 0)
    own_value = own.astype(F32)
    for t in range(4):
        outer_rank = jnp.where(rows[t : t + 1] < 0, counts[t : t + 1], -1)
        outer_ref[t] = one_hot(outer_rank == slot)
        face_row = rows[4 + t : 5 + t]
        shared_rank = jnp.where(face_row < 0, -1, lane - counts[4 + t : 5 + t])
        wanted = jnp.sum(
            jnp.where(shared_rank == slot, face_row.astype(F32), 0.0), axis=1, keepdims=True
        )
        face_ref[128 * t : 128 * t + 128, :] = one_hot(own_value == wanted)
    count = prefix_counts(jnp.broadcast_to(local, (8, 64)))[0:1]
    target = jnp.where(local < 0, 32 + count, iota((1, 64), 1) - count)
    return one_hot(target == iota((64, 64), 0))


def select_rows(parts, row_hot):
    stack = []
    for value in parts:
        for piece in split(value):
            stack.append(dot(row_hot, piece).astype(BF16))
    return jnp.concatenate(stack, axis=0)


def joined(stack):
    return [stack[0:64] + stack[64:128], stack[128:192] + stack[192:256]]


def pick(par, former, latter):
    return jnp.where(par == 0, former, latter)


def complex_product(x, w):
    m = x[0].shape[0]
    hi, lo = split(jnp.concatenate(x, axis=0))
    both = jnp.concatenate([hi, lo], axis=0)
    sums = []
    for part in range(2):
        main = dot(both, w[0, part])
        sums.append(main[: 2 * m] + main[2 * m :] + dot(hi, w[1, part]))
    by_real, by_imag = sums
    return [by_real[:m] - by_imag[m:], by_imag[:m] + by_real[m:]]


def convert(fetch, pieces):
    @pl.loop(0, RING)
    def _(k):
        rows = pl.ds(pl.multiple_of(k * 32, 32), 32)
        for part in range(2):
            hi, lo = split(fetch(k, part))
            pieces[0, part, rows, :] = hi
            pieces[1, part, rows, :] = lo


def weave(alpha, beta):
    return jnp.concatenate([alpha[0:16], beta[0:16], alpha[16:32], beta[16:32]], axis=0)


def kernel(
    maps_ref, faces_ref, parent_out, grand_ref,
    maps, child_rows, parent_rows, parent_ref,
    ss1, sx1a, sx1b, xs1, xx1, ss2, sx2, xs2, xx2, out_ss, out_sx, out_xs, out_xx, out_sx2, out_xx2,
    face_hot, outer_hot, face_hot2, outer_hot2, place_hot, wss, wsx, wsx2, send, recv, local_sem,
):
    box, row = lax.axis_index("box"), lax.axis_index("row")
    par = lax.rem(box, 2)
    mate = box + 1 - 2 * par
    core = lax.rem(row, 2)
    z = lax.div(row, 2)
    sib = row + 1 - 2 * core
    up, down = lax.rem(row + 2, RING), lax.rem(row + RING - 2, RING)
    to_up, to_down, to_sib, to_mate = (box, up), (box, down), (box, sib), (mate, row)

    barrier = pltpu.get_barrier_semaphore()
    for target in (to_up, to_down, to_sib, to_mate):
        pl.semaphore_signal(barrier, inc=1, device_id=target, device_id_type=MESH)

    first = 2 * (box - par)

    def group(i):
        return pl.ds(pl.multiple_of(8 * lax.div(i, 8), 8), 8)

    loads = [
        pltpu.make_async_copy(faces_ref.at[group(first)], child_rows, local_sem.at[0]),
        pltpu.make_async_copy(maps_ref.at[:, 1 - par], maps.at[1], local_sem.at[1]),
        pltpu.make_async_copy(maps_ref.at[:, par], maps.at[0], local_sem.at[2]),
        pltpu.make_async_copy(faces_ref.at[group(32 + box)], parent_rows, local_sem.at[3]),
    ]
    for c in loads:
        c.start()

    ids = {}
    pending = []

    def copy(src, dst, target, key):
        k = ids.setdefault(key, len(ids))
        return pltpu.make_async_remote_copy(
            src_ref=src, dst_ref=dst, send_sem=send.at[k], recv_sem=recv.at[k],
            device_id=target, device_id_type=MESH,
        )

    def push(src, dst, target, key):
        c = copy(src, dst, target, key)
        c.start()
        pending.append(c)

    def drain(spare):
        while len(pending) > spare:
            pending.pop(0).wait_send()

    def arrived(dst, key):
        copy(dst, dst, to_mate, key).wait_recv()

    def away(base, way, hops):
        return lax.rem(base + 2 * RING + (2 if way else -2) * hops, RING)

    class Section:
        settled = -1

        def __init__(self, name, buf, part=None, forward=False, source=None):
            self.name, self.buf, self.part, self.forward, self.source = name, buf, part, forward, source

        def block(self, slot):
            return self.buf.at[slot] if self.part is None else self.buf.at[slot, self.part]

        def piece(self, base, way, hop):
            slot = away(base, way, hop)
            if hop < 3:
                return self.block(slot)
            if self.part is not None:
                return self.buf.at[slot, self.part, pl.ds(16 * way, 16)]
            return self.buf.at[slot, way]

        def to_mate(self, slot, what):
            if self.forward:
                block = self.block(slot)
                push(block, block, to_mate, (self.name, "mate", what))

        def send(self, way, hop):
            if hop == 0 and way == 0 and self.source is not None:
                arrived(*self.source)
            piece = self.piece(row, way, hop)
            push(piece, piece, to_down if way else to_up, (self.name, way, hop))
            if hop == 0 and way == 1:
                own = self.block(row)
                push(own, own, to_sib, (self.name, "sib", "own"))
                self.to_mate(row, "own")

        def receive(self, way, hop):
            slot = away(row, way, hop + 1)
            if hop < 3:
                piece = self.block(slot)
            else:
                piece = self.piece(away(row, way, 1), way, hop)
            arrived(piece, (self.name, way, hop))
            return slot, piece

        def share(self, way, hop, slot, piece):
            push(piece, piece, to_sib, (self.name, "sib", way, hop))
            if hop < 3:
                self.to_mate(slot, (way, hop))
            elif way == 1:
                self.to_mate(slot, "far")

        def settle(self, hop):
            while self.settled <= hop:
                if self.settled < 0:
                    arrived(self.block(sib), (self.name, "sib", "own"))
                else:
                    for way in range(2):
                        if self.settled < 3:
                            piece = self.block(away(sib, way, self.settled + 1))
                        else:
                            piece = self.piece(away(sib, way, 1), way, 3)
                        arrived(piece, (self.name, "sib", way, self.settled))
                self.settled += 1

        def done(self):
            self.settle(3)

    class Flow:
        def __init__(self, order, depth):
            self.order, self.depth = order, depth
            self.sent = self.got = 0

        def ready(self, got):
            more = []
            while self.sent < len(self.order) and self.sent < got + self.depth:
                section, hop = self.order[self.sent]
                if hop and (section, hop - 1) not in self.order[:got]:
                    break
                more.append((section, hop))
                self.sent += 1
            return more

        def begin(self):
            for section, hop in self.ready(self.got):
                for way in range(2):
                    section.send(way, hop)

        def extend(self, order):
            self.order += order
            self.begin()

        def advance(self, upto=None):
            upto = self.got + 1 if upto is None else upto
            while self.got < min(upto, len(self.order)):
                section, hop = self.order[self.got]
                following = self.ready(self.got + 1)
                now = [pair for pair in following if pair[1]]
                shared = []
                for way in range(2):
                    shared.append((way, hop, *section.receive(way, hop)))
                    for later, later_hop in now:
                        later.send(way, later_hop)
                for one in shared:
                    section.share(*one)
                for later, later_hop in following:
                    for way in range(2):
                        if not later_hop:
                            later.send(way, later_hop)
                section.settle(hop - 1)
                self.got += 1

        def through(self, section):
            return self.order.index((section, 3)) + 1

    class Mirror:
        def __init__(self, name, mine, buf):
            self.name, self.mine, self.buf = name, mine, buf

        def block(self, slot):
            return self.buf.at[slot, 1]

        def take(self, slot, what):
            block = self.block(slot)
            arrived(block, (self.mine, "mate", what))
            push(block, block, to_sib, (self.name, "sib", what))

        def start(self):
            self.take(row, "own")

        def step(self, j):
            for way in range(2):
                self.take(away(row, way, j + 1), (way, j))
            self.settle(j - 1)

        def last(self):
            self.take(away(row, 0, 4), "far")
            self.settle(2)

        def settle(self, j):
            if j < 0:
                arrived(self.block(sib), (self.name, "sib", "own"))
            else:
                for way in range(2):
                    arrived(self.block(away(sib, way, j + 1)), (self.name, "sib", (way, j)))

        def done(self):
            arrived(self.block(away(sib, 0, 4)), (self.name, "sib", "far"))

    def faces_of(rows, i):
        inside = lax.rem(i, 8)
        lanes = pl.ds(pl.multiple_of(z * 128, 128), 128)
        whole = jnp.sum(
            jnp.where(iota((8, ORDER), 0) == inside, rows[...], 0), axis=0, keepdims=True
        )
        chunk = jnp.sum(
            jnp.where(iota((8, 128), 0) == inside, rows[:, lanes], 0), axis=0, keepdims=True
        )
        local = jnp.where(core == 0, chunk[:, :64], chunk[:, 64:])
        return whole, local

    def select(child, own_index, pair_index):
        own_faces, local = faces_of(child_rows, own_index)
        paired, _ = faces_of(child_rows, pair_index)
        hot = build_selectors(own_faces, paired, local, face_hot, outer_hot)
        loads[2 - child].wait()
        stack = select_rows([maps[child, part] for part in range(2)], hot)
        face = joined(dot_nt(stack, face_hot[...]))
        outer = jnp.concatenate(
            [dot_nt(stack[:, 256 * t : 256 * t + 256], outer_hot[t]) for t in range(4)], axis=1
        )
        return face, joined(outer)

    loads[0].wait()
    face, outer = select(1, first + 1 + par, first + 3 - 3 * par)
    for part in range(2):
        out_ss[part] = face[part][:32]
        out_xs[part] = face[part][32:]
        out_xx[part] = outer[part][32:]
        halves = [outer[part][:32, :256], outer[part][:32, 256:]]
        out_sx[0, part] = pick(par, halves[1], halves[0])
        out_sx[1, part] = pick(par, halves[0], halves[1])
    pl.semaphore_wait(barrier, 4)
    push(out_ss, ss1.at[par, row], to_mate, "ss1")

    face, outer = select(0, first + 3 * par, first + 2 - par)
    for part in range(2):
        ss1[par, row, part] = face[part][:32]
        xs1[par, part] = face[part][32:]
        xx1[par, part] = outer[part][32:]
        halves = [outer[part][:32, :256], outer[part][:32, 256:]]
        sx1a[row, par, part] = pick(par, halves[0], halves[1])
        sx1b[par, row, part] = pick(par, halves[1], halves[0])
    ssm = Section("ssm1", ss1.at[par])
    sso = Section("sso1", ss1.at[1 - par], source=(ss1.at[1 - par, row], "ss1"))
    xa = Section("sxa1", sx1a, source=(sx1a.at[row, 1 - par], "mate sxa1"))
    mb = Section("sxm1", sx1b.at[par])
    ob = Section("sxo1", sx1b.at[1 - par], source=(sx1b.at[1 - par, row], "mate sxb1"))
    flow = Flow(order_parent(ssm, sso, xa, mb, ob), 2)
    flow.begin()
    push(out_sx.at[0], sx1a.at[row, par], to_mate, "mate sxa1")
    flow.depth = DEPTHS[0]
    flow.begin()

    def horner(ss, xs, more):
        convert(lambda k, part: ss[1, k, part], wss.at[1])
        u = [xs[0, part] for part in range(2)]
        lead = complex_product(u, wss.at[1])
        base = [jnp.concatenate([lead[part], -xs[1, part]], axis=0) for part in range(2)]
        more()
        convert(lambda k, part: ss[0, k, part], wss.at[0])
        w = base
        for term in range(3):
            t = complex_product(w, wss.at[0])
            more()
            t = complex_product(t, wss.at[1])
            w = [base[part] + t[part] for part in range(2)]
            more()
        t = complex_product(w, wss.at[0])
        t = [jnp.concatenate([t[part][:32] + u[part], t[part][32:]], axis=0) for part in range(2)]
        return w, t

    rank, place = iota((256, 256), 0), iota((256, 256), 1)
    inside = jnp.where(rank < 128, rank, rank - 128)
    spot = 32 * lax.div(inside, 16) + lax.rem(inside, 16) + jnp.where(rank < 128, 0, 16)
    place_hot[...] = one_hot(spot == place)

    def finish(w, t, wx, xx):
        alpha, beta = complex_product(w, wx.at[0]), complex_product(t, wx.at[1])
        tiles = []
        for part in range(2):
            left = weave(xx[0][part] + alpha[part][:32], alpha[part][32:])
            right = weave(-beta[part][:32], xx[1][part] - beta[part][32:])
            tiles.append((left, right))
        columns = []
        for tile in range(2):
            cols = slice(128 * tile, 128 * tile + 128)
            packed = jnp.concatenate(
                [jnp.concatenate([left[:, cols], right[:, cols]], axis=1) for left, right in tiles],
                axis=0,
            )
            hi, lo = split(packed)
            spread = dot(jnp.concatenate([hi, lo], axis=0), place_hot[...])
            columns.append(spread[:128] + spread[128:])
        both = jnp.concatenate(columns, axis=1)
        return [both[:64], both[64:]]

    loads[3].wait()
    own, loc = faces_of(parent_rows, box)
    pair, _ = faces_of(parent_rows, mate)
    hot2 = build_selectors(own, pair, loc, face_hot2, outer_hot2)
    flow.advance(2)
    push(out_sx.at[1], sx1b.at[par, row], to_mate, "mate sxb1")
    flow.advance(3)
    push(out_xs, xs1.at[par], to_mate, "xs1")
    push(out_xx, xx1.at[par], to_mate, "xx1")
    flow.advance(max(flow.through(ssm), flow.through(sso)))
    arrived(xs1.at[1 - par], "xs1")
    arrived(xx1.at[1 - par], "xx1")
    ssm.done()
    sso.done()
    w, t = horner(ss1, xs1, lambda: flow.advance(min(flow.got + 1, flow.through(xa))))

    ssi, ssr = Section("ssi2", ss2.at[par], part=1, forward=True), Section("ssr2", ss2.at[par], part=0)
    sso = Section("sso2", ss2.at[1 - par], part=0, source=(ss2.at[1 - par, row, 0], "ss2"))
    mirror = Mirror("mir2", "ssi2", ss2.at[1 - par])
    sxm = Section("sxm2", sx2.at[par])
    sxo = Section("sxo2", sx2.at[1 - par], source=(sx2.at[1 - par, row], "sx2"))
    face = jnp.zeros((256, 512), F32)
    for h in range(2):
        side = par if h == 0 else 1 - par
        lanes = pl.ds(pl.multiple_of(256 * side, 256), 256)
        if h == 0:
            flow.advance(flow.through(xa))
            xa.done()
        else:
            flow.advance(max(flow.through(mb), flow.through(ob)) + 1)
            mb.done()
            ob.done()
        for role in range(2):
            if h == 0:
                convert(lambda k, part: sx1a[k, role, part], wsx.at[h, role])
            else:
                convert(lambda k, part: sx1b[role, k, part], wsx.at[h, role])
        xx = [[xx1[role, part, :, lanes] for part in range(2)] for role in range(2)]
        merged = finish(w, t, wsx.at[h], xx)
        wide = pl.ds(pl.multiple_of(512 * side, 512), 512)
        for part in range(2):
            parent_ref[part, :, wide] = merged[part]
        stack = select_rows(merged, hot2)
        outer = joined(
            jnp.concatenate(
                [dot_nt(stack[:, 256 * i : 256 * i + 256], outer_hot2[2 * side + i]) for i in range(2)],
                axis=1,
            )
        )
        if h == 0:
            for part in range(2):
                sx2[par, row, part] = outer[part][:32]
                xx2[par, part] = outer[part][32:]
            flow.extend([(sxm, 0), (sxm, 1)])
        face = face + dot_nt(stack, face_hot2[:, wide])
    face = joined(face)
    for part in range(2):
        ss2[par, row, part] = face[part][:32]
        xs2[par, part] = face[part][32:]
    real = ss2.at[par, row, 0]
    push(real, real, to_mate, "ss2")
    flow.depth = DEPTHS[1]
    flow.extend(order_grand(ssi, ssr, sso, sxm, sxo))
    for part in range(2):
        out_sx2[part] = outer[part][:32]
        out_xx2[part] = outer[part][32:]
    push(out_sx2, sx2.at[par, row], to_mate, "sx2")
    store = pltpu.make_async_copy(parent_ref, parent_out.at[:, 0], local_sem.at[4])
    store.start()
    drain(30)
    at = [flow.order.index((ssi, hop)) + 1 for hop in range(4)]
    flow.advance(at[0])
    push(xs2.at[par], xs2.at[par], to_mate, "xs2")
    mirror.start()
    flow.advance(at[1])
    mirror.step(0)
    push(out_xx2, xx2.at[par], to_mate, "xx2")
    flow.advance(at[2])
    mirror.step(1)
    flow.advance(max(flow.through(ssi), flow.through(ssr), flow.through(sso)))
    mirror.step(2)
    mirror.last()
    arrived(xs2.at[1 - par], "xs2")
    arrived(xx2.at[1 - par], "xx2")
    flow.advance()
    ssi.done()
    ssr.done()
    sso.done()
    mirror.done()
    w, t = horner(ss2, xs2, flow.advance)
    drain(16)
    flow.advance(len(flow.order))
    sxm.done()
    sxo.done()
    for role in range(2):
        convert(lambda k, part: sx2[role, k, part], wsx2.at[role])
    xx = [[xx2[role, part] for part in range(2)] for role in range(2)]
    merged = finish(w, t, wsx2, xx)
    for part in range(2):
        grand_ref[part] = merged[part]

    store.wait()
    drain(0)
    assert len(ids) <= TOTAL


def per_device(child_maps, child_faces, parent_faces):
    def vmem(*shape, dtype=F32):
        return pltpu.VMEM(shape, dtype)

    whole = pl.BlockSpec(memory_space=pltpu.VMEM)
    placed = pl.BlockSpec(memory_space=pltpu.HBM)
    return pl.pallas_call(
        kernel,
        out_shape=(
            jax.ShapeDtypeStruct((2, 1, 64, ORDER), F32),
            jax.ShapeDtypeStruct((2, 64, SHARED), F32),
        ),
        in_specs=[placed] * 2,
        out_specs=(placed, whole),
        scratch_shapes=[
            vmem(2, 2, 64, ORDER), pltpu.VMEM((8, ORDER), jnp.int32), pltpu.VMEM((8, ORDER), jnp.int32),
            vmem(2, 64, ORDER),
            vmem(2, RING, 2, 32, 512), vmem(RING, 2, 2, 32, 256), vmem(2, RING, 2, 32, 256), vmem(2, 2, 32, 512), vmem(2, 2, 32, 512),
            vmem(2, RING, 2, 32, 512), vmem(2, RING, 2, 32, 256), vmem(2, 2, 32, 512), vmem(2, 2, 32, 256),
            vmem(2, 32, 512), vmem(2, 2, 32, 256), vmem(2, 32, 512), vmem(2, 32, 512),
            vmem(2, 32, 256), vmem(2, 32, 256),
            vmem(512, 1024, dtype=BF16), vmem(4, 128, 256, dtype=BF16),
            vmem(512, 1024, dtype=BF16), vmem(4, 128, 256, dtype=BF16),
            vmem(256, 256, dtype=BF16),
            vmem(2, 2, 2, 512, 512, dtype=BF16),
            vmem(2, 2, 2, 2, 512, 256, dtype=BF16),
            vmem(2, 2, 2, 512, 256, dtype=BF16),
            pltpu.SemaphoreType.DMA((TOTAL,)),
            pltpu.SemaphoreType.DMA((TOTAL,)),
            pltpu.SemaphoreType.DMA((5,)),
        ],
        compiler_params=pltpu.CompilerParams(
            collective_id=0, has_side_effects=True, vmem_limit_bytes=54000 * 1024
        ),
    )(child_maps, jnp.concatenate([child_faces, parent_faces], axis=0))


def solution(mesh):
    placed = (P(None, "box", "row", None), P(), P())
    return jax.shard_map(
        per_device,
        mesh=mesh,
        in_specs=placed,
        out_specs=(P(None, "box", "row", None), P(None, "row", "box")),
        check_vma=False,
    )
```
